128 devices in a mesh: dp: 4 (over z_hi, core), seq: 32 (over x, z_lo, y).
Axes of the slice: x: 4, y: 4, z: 4 (z_hi: 2, z_lo: 2; z = z_hi * 2 + z_lo), core: 2. Of those that a mesh axis runs over, the one named last changes fastest.
Arguments:
- frames_in: bfloat16 [384, 256, 1152], P(('dp', 'seq')), parts along dimension 0, may hold values from -18 to 18
- modulation: float32 [12, 1152], P('dp'), parts along dimension 0, may hold values from -3 to 3
- caption_kv: bfloat16 [480, 2304], P('dp', 'seq'), parts along dimension 0, may hold values from -18 to 18
- caption_len: int32 [4], P('dp'), parts along dimension 0, may hold values from 30 to 120
- w_spatial_qkv: bfloat16 [1152, 3456], replicated, may hold values from -0.1875 to 0.1875
- w_spatial_proj: bfloat16 [1152, 1152], replicated, may hold values from -0.1875 to 0.1875
- w_temporal_qkv: bfloat16 [1152, 3456], replicated, may hold values from -0.1875 to 0.1875
- w_temporal_proj: bfloat16 [1152, 1152], replicated, may hold values from -0.1875 to 0.1875
- w_cross_q: bfloat16 [1152, 1152], P('seq'), may hold values from -0.1875 to 0.1875
- w_cross_out: bfloat16 [1152, 1152], P('seq'), may hold values from -0.1875 to 0.1875
Outputs:
- block_out: bfloat16 [384, 256, 1152], P(('dp', 'seq')), parts along dimension 0
The draws below stay inside these ranges and needn't reach their ends.
There are 4 independent parts, one for each index of `dp`. The reference program is written for one: setup_inputs(seed, part) draws one part's arguments, and reference() takes and returns one part's arrays. A program takes and returns all parts, laid end to end along the dimension named above; an argument that names none is the same for every part. Nothing has to cross between parts.
Inputs may be any that keep to these rules, and one draw needn't show every extreme that they name: At least a quarter of the 120 caption slots are valid; slots from caption_len on are padding.
All inputs are finite; a program needn't handle non-finite values.
Results may differ from the reference program's by a relative error of at most 0.034.
Values may be sent and summed in bfloat16 or wider, within the bound.
A program may use at most 128 MiB of HBM per device.

```python
import jax
import jax.numpy as jnp
from jax import lax

D = 1152
HEADS = 16
HEAD = 72
CAP = 120
FRAMES = 96
PATCHES = 256


def draw_frames_in(key, part):
    key = jax.random.fold_in(key, 11)
    return jnp.clip(jax.random.normal(key, (FRAMES, PATCHES, D), jnp.float32), -6.0, 6.0).astype(jnp.bfloat16)


def draw_modulation(key, part):
    key = jax.random.fold_in(key, 12)
    first_key, second_key, third_key = jax.random.split(key, 3)
    offset_row = jnp.clip(0.5 * jax.random.normal(first_key, (1, D), jnp.float32), -3.0, 3.0)
    scale_row = jnp.clip(0.5 * jax.random.normal(second_key, (1, D), jnp.float32), -3.0, 3.0)
    gate_row = jnp.clip(jax.random.normal(third_key, (1, D), jnp.float32), -3.0, 3.0)
    return jnp.concatenate([offset_row, scale_row, gate_row], axis=0)


def draw_caption_kv(key, part):
    key = jax.random.fold_in(key, 13)
    return jnp.clip(jax.random.normal(key, (CAP, 2 * D), jnp.float32), -6.0, 6.0).astype(jnp.bfloat16)


def block_scale(rng, dims, cuts, low, high):
    gain, own = 1.0, jax.random.fold_in(rng, 6)
    for position, blocks in cuts:
        heights = jnp.exp(jax.random.uniform(jax.random.fold_in(own, position), (blocks,), jnp.float32, low / len(cuts), high / len(cuts)))
        gain = gain * jnp.repeat(heights, dims[position] // blocks).reshape([-1 if axis == position else 1 for axis in range(len(dims))])
    return gain


def normal_values(stream_key, shape, spread, bound, shards=(), kind=jnp.bfloat16):
    array = spread * jax.random.normal(stream_key, shape, jnp.float32)
    if shards:
        array = array * block_scale(stream_key, shape, shards, -0.22, 0.18)
    return jnp.clip(array, -bound, bound).astype(kind)


def setup_inputs(seed: int = 0, part: int = 0) -> dict:
    key_of = jax.random.split(jax.random.key(seed), 11)
    part_keys = jax.random.split(jax.random.fold_in(key_of[10], part), 11)
    return {
        "frames_in": draw_frames_in(jax.random.fold_in(jax.random.fold_in(key_of[10], part), 71), part),
        "modulation": draw_modulation(jax.random.fold_in(jax.random.fold_in(key_of[10], part), 71), part),
        "caption_kv": draw_caption_kv(jax.random.fold_in(jax.random.fold_in(key_of[10], part), 71), part),
        "caption_len": jax.random.randint(part_keys[3], (1,), CAP // 4, CAP + 1).astype(jnp.int32),
        "w_spatial_qkv": normal_values(key_of[4], (D, 3 * D), D ** -0.5, 0.1875),
        "w_spatial_proj": normal_values(key_of[5], (D, D), D ** -0.5, 0.1875),
        "w_temporal_qkv": normal_values(key_of[6], (D, 3 * D), D ** -0.5, 0.1875),
        "w_temporal_proj": normal_values(key_of[7], (D, D), D ** -0.5, 0.1875),
        "w_cross_q": normal_values(key_of[8], (D, D), D ** -0.5, 0.1875, ((0, 32),)),
        "w_cross_out": normal_values(key_of[9], (D, D), D ** -0.5, 0.1875, ((0, 32),)),
    }


def layer_normed(inputs):
    widened = inputs.astype(jnp.float32)
    centered = widened - lax.optimization_barrier(jnp.mean(widened, axis=-1, keepdims=True))
    variance = lax.optimization_barrier(jnp.mean(centered * centered, axis=-1, keepdims=True))
    return centered * lax.rsqrt(variance + 1e-06)

def attend(queries, key_rows, value_rows, allowed):
    count_q = queries.shape[0]
    count_k = key_rows.shape[0]
    q_heads = queries.astype(jnp.float32).reshape(count_q, HEADS, HEAD)
    k_heads = key_rows.astype(jnp.float32).reshape(count_k, HEADS, HEAD)
    v_heads = value_rows.astype(jnp.float32).reshape(count_k, HEADS, HEAD)
    scores = jnp.einsum('qhe,khe->hqk', q_heads, k_heads) * HEAD ** (-0.5)
    scores = jnp.where(allowed[None, None, :], scores, -jnp.inf)
    maximum = lax.optimization_barrier(jnp.max(scores, axis=-1, keepdims=True))
    exponent = jnp.exp(scores - maximum)
    weights = (exponent / lax.optimization_barrier(jnp.sum(exponent, axis=-1, keepdims=True))).astype(jnp.bfloat16)
    mixture = jnp.einsum('hqk,khe->qhe', weights.astype(jnp.float32), v_heads)
    return mixture.reshape(count_q, HEADS * HEAD).astype(jnp.bfloat16)

def reference(frames_in, modulation, caption_kv, caption_len, w_spatial_qkv, w_spatial_proj, w_temporal_qkv, w_temporal_proj, w_cross_q, w_cross_out):
    offset_row = modulation[0]
    scale_row = modulation[1]
    gate_row = modulation[2]
    every_patch = jnp.ones((PATCHES,), dtype=bool)
    every_frame = jnp.ones((FRAMES,), dtype=bool)
    allowed = jnp.arange(CAP, dtype=jnp.int32) < caption_len[0]
    caption_keys = caption_kv[:, :D]
    caption_values = caption_kv[:, D:]

    def spatial_frame(frame):
        modulated = (layer_normed(frame) * (1.0 + scale_row) + offset_row).astype(jnp.bfloat16)
        qkv_rows = jnp.dot(modulated, w_spatial_qkv, preferred_element_type=jnp.float32).astype(jnp.bfloat16)
        mixture = attend(qkv_rows[:, :D], qkv_rows[:, D:2 * D], qkv_rows[:, 2 * D:], every_patch)
        branch = jnp.dot(mixture, w_spatial_proj, preferred_element_type=jnp.float32)
        return (frame.astype(jnp.float32) + gate_row * branch).astype(jnp.bfloat16)
    after_spatial = lax.map(spatial_frame, frames_in)

    def temporal_patch(column):
        qkv_rows = jnp.dot(column, w_temporal_qkv, preferred_element_type=jnp.float32).astype(jnp.bfloat16)
        mixture = attend(qkv_rows[:, :D], qkv_rows[:, D:2 * D], qkv_rows[:, 2 * D:], every_frame)
        branch = jnp.dot(mixture, w_temporal_proj, preferred_element_type=jnp.float32)
        return (column.astype(jnp.float32) + gate_row * branch).astype(jnp.bfloat16)
    after_temporal = jnp.swapaxes(lax.map(temporal_patch, jnp.swapaxes(after_spatial, 0, 1)), 0, 1)

    def cross_frame(frame):
        queries = jnp.dot(frame, w_cross_q, preferred_element_type=jnp.float32).astype(jnp.bfloat16)
        mixture = attend(queries, caption_keys, caption_values, allowed)
        branch = jnp.dot(mixture, w_cross_out, preferred_element_type=jnp.float32)
        return (frame.astype(jnp.float32) + branch).astype(jnp.bfloat16)
    return lax.map(cross_frame, after_temporal)
```

```python
import functools
import math

import jax
import jax.numpy as jnp
from jax import lax
from jax.experimental import pallas as pl
from jax.experimental.pallas import tpu as pltpu
from jax.sharding import PartitionSpec as P

HEADS = 16
HEAD = 72
D = 1152
LANES = 128
SPAN = 128
SEQ = 32
LOCAL = 3
PATCH = 8
CAP = 120
ROWS = 256
BF = jnp.bfloat16
F32 = jnp.float32
MESH = pl.DeviceIdType.MESH
EXP_SCALE = HEAD ** (-0.5) * math.log2(math.e)
COLS = 384


def window(head):
    low = HEAD * head
    return low // LANES * LANES, -(-(low + HEAD) // LANES) * LANES


def dot_nt(a, b):
    return lax.dot_general(a, b, (((1,), (1,)), ((), ())), preferred_element_type=F32)


def dot_nn(a, b):
    return jnp.dot(a, b, preferred_element_type=F32)


def head_mask(head):
    first, last = window(head)
    lane = lax.broadcasted_iota(jnp.int32, (1, last - first), 1) + first
    return jnp.where((lane >= HEAD * head) & (lane < HEAD * (head + 1)), 1.0, 0.0).astype(BF)


def placed(head):
    first, last = window(head)
    shape = (LANES, last - first)
    feature = lax.broadcasted_iota(jnp.int32, shape, 0)
    lane = lax.broadcasted_iota(jnp.int32, shape, 1) + first
    return jnp.where((lane == feature + HEAD * head) & (feature < HEAD), 1.0, 0.0).astype(BF)


def frame_to_patch():
    row = lax.broadcasted_iota(jnp.int32, (ROWS, ROWS), 0)
    column = lax.broadcasted_iota(jnp.int32, (ROWS, ROWS), 1)
    return jnp.where(column == (row % SEQ) * PATCH + row // SEQ, 1.0, 0.0).astype(BF)


def patch_to_frame():
    row = lax.broadcasted_iota(jnp.int32, (ROWS, ROWS), 0)
    column = lax.broadcasted_iota(jnp.int32, (ROWS, ROWS), 1)
    return jnp.where(column == (row % PATCH) * SEQ + row // PATCH, 1.0, 0.0).astype(BF)


def attend_t(queries, keys, values_t):
    scores = dot_nt(keys, queries)
    top = jnp.max(scores, axis=0, keepdims=True)
    weights = jnp.exp2((scores - top) * EXP_SCALE)
    total = jnp.sum(weights, axis=0, keepdims=True)
    return dot_nn(values_t, weights.astype(BF)) * (1.0 / total)


def kernel(
    caption_len, frames_ref, modulation, caption_ref, wsqkv_ref, wsp_ref, wtqkv_ref, wtp_ref, wc_ref,
    out_ref,
    frames, wsqkv, wsp, wtqkv, wtp, wy, wg, cap, cap_scores, cap_values,
    modulated, qk, vt, mix_t, mix, sent, received, x, tqk, tv, tvt, tmix_t, tmix, weights_n,
    load_sem, y_send, y_recv, g_send, g_recv, s_send, s_recv, c_send, c_recv, f_send, f_recv, r_send, r_recv, local_sem,
):
    me = lax.axis_index("seq")
    dp = lax.axis_index("dp")
    core = dp % 2
    my_y = me % 4
    my_block = me // 4

    def peer_of(k):
        y = (me % 4 + k % 4) % 4
        x_ = (me // 8 + (k // 4) % 4) % 4
        z = (me // 4 + k // 16) % 2
        return x_ * 8 + z * 4 + y

    barrier = pltpu.get_barrier_semaphore()

    @pl.loop(1, SEQ)
    def _(k):
        pl.semaphore_signal(barrier, inc=1, device_id={"seq": peer_of(k)}, device_id_type=MESH)

    pl.semaphore_signal(barrier, inc=1, device_id={"dp": dp + 1 - 2 * core}, device_id_type=MESH)

    loads = [
        pltpu.make_async_copy(frames_ref, frames, load_sem.at[0]),
        pltpu.make_async_copy(wsqkv_ref.at[:, :D], wsqkv.at[:, :D], load_sem.at[1]),
        pltpu.make_async_copy(wsqkv_ref.at[:, D : 2 * D], wsqkv.at[:, D : 2 * D], load_sem.at[2]),
        pltpu.make_async_copy(wsqkv_ref.at[:, 2 * D :], wsqkv.at[:, 2 * D :], load_sem.at[3]),
        pltpu.make_async_copy(wsp_ref, wsp, load_sem.at[4]),
        pltpu.make_async_copy(wtqkv_ref, wtqkv, load_sem.at[5]),
        pltpu.make_async_copy(wtp_ref, wtp, load_sem.at[6]),
    ]
    for load in loads:
        load.start()
    own_caption = pltpu.make_async_copy(caption_ref, cap.at[me], local_sem.at[0])
    own_caption.start()
    own_weight = pltpu.make_async_copy(wc_ref.at[core], wy.at[my_y], local_sem.at[1])
    own_weight.start()

    pl.semaphore_wait(barrier, SEQ)

    @pl.loop(1, 4)
    def _(k):
        y = (my_y + k) % 4
        pltpu.make_async_remote_copy(
            wc_ref.at[core], wy.at[my_y], y_send, y_recv, device_id={"seq": my_block * 4 + y}, device_id_type=MESH
        ).start()

    @pl.loop(1, SEQ)
    def _(k):
        pltpu.make_async_remote_copy(
            caption_ref, cap.at[me], c_send, c_recv, device_id={"seq": peer_of(k)}, device_id_type=MESH
        ).start()

    def block_peer(k):
        x_ = (me // 8 + k % 4) % 4
        z = (me // 4 + k // 4) % 2
        return x_ * 8 + z * 4 + my_y

    def gather_blocks():
        own_weight.wait()
        pltpu.make_async_copy(wy.at[pl.ds(0, 3)], wy.at[pl.ds(0, 3)], y_recv).wait()
        for c in range(0, D, COLS):
            total = None
            for y in range(4):
                row = lax.broadcasted_iota(jnp.int32, (144, 36), 0)
                column = lax.broadcasted_iota(jnp.int32, (144, 36), 1)
                place = jnp.where(row == column + 36 * y, 1.0, 0.0).astype(BF)
                term = dot_nn(place, wy[y, :, c : c + COLS])
                total = term if total is None else total + term
            wg[core, my_block, :, c : c + COLS] = total.astype(BF)

        @pl.loop(1, 8)
        def _(k):
            pltpu.make_async_remote_copy(
                wg.at[core, my_block], wg.at[core, my_block], g_send, g_recv,
                device_id={"seq": block_peer(k)}, device_id_type=MESH,
            ).start()

    def swap_copy():
        return pltpu.make_async_remote_copy(
            wg.at[core], wg.at[core], s_send, s_recv, device_id={"dp": dp + 1 - 2 * core}, device_id_type=MESH
        )

    def swap_weights():
        pltpu.make_async_copy(wg.at[core, pl.ds(0, 7)], wg.at[core, pl.ds(0, 7)], g_recv).wait()
        swap_copy().start()

    def spatial(f, _):
        @pl.when(f == 0)
        def _():
            loads[0].wait()

        @pl.loop(0, ROWS // 32)
        def _(r):
            rows = pl.ds(pl.multiple_of(r * 32, 32), 32)
            wide = frames[f, rows, :].astype(F32)
            centered = wide - jnp.mean(wide, axis=-1, keepdims=True)
            variance = jnp.mean(centered * centered, axis=-1, keepdims=True)
            normed = centered * lax.rsqrt(variance + 1e-06)
            modulated[rows, :] = (normed * (1.0 + modulation[1:2, :]) + modulation[0:1, :]).astype(BF)

        for part in range(3):
            @pl.when(f == 0)
            def _():
                loads[1 + part].wait()

            for c in range(0, D, COLS):
                product = dot_nn(modulated[...], wsqkv[:, part * D + c : part * D + c + COLS])
                if part < 2:
                    qk[:, part * D + c : part * D + c + COLS] = product.astype(BF)
                else:
                    vt[c : c + COLS, :] = product.T

        for head in range(HEADS):
            first, last = window(head)
            keys = qk[:, D + first : D + last] * head_mask(head)
            values_t = vt[HEAD * head : HEAD * (head + 1), :].astype(BF)
            mix_t[HEAD * head : HEAD * (head + 1), :] = attend_t(qk[:, first:last], keys, values_t)

        for c in range(0, D, COLS):
            mix[:, c : c + COLS] = mix_t[c : c + COLS, :].T.astype(BF)

        @pl.when(f == 0)
        def _():
            loads[4].wait()

        for c in range(0, D, COLS):
            branch = dot_nn(mix[...], wsp[:, c : c + COLS])
            after = frames[f, :, c : c + COLS].astype(F32) + modulation[2:3, c : c + COLS] * branch
            sent[f, :, :, c : c + COLS] = after.reshape(SEQ, PATCH, COLS).astype(BF)

        @pl.loop(1, SEQ)
        def _(k):
            peer = peer_of(k)
            pltpu.make_async_remote_copy(
                sent.at[f, peer], received.at[f, me], f_send.at[f], f_recv.at[f],
                device_id={"seq": peer}, device_id_type=MESH,
            ).start()

        received[f, me] = sent[f, me]

        @pl.when(f == 0)
        def _():
            gather_blocks()

        @pl.when(f == 1)
        def _():
            swap_weights()

        return 0

    lax.fori_loop(0, LOCAL, spatial, 0)

    def temporal_qkv(f, _):
        pltpu.make_async_copy(
            received.at[f, pl.ds(0, SEQ - 1)], received.at[f, pl.ds(0, SEQ - 1)], f_recv.at[f]
        ).wait()

        @pl.when(f == 0)
        def _():
            loads[5].wait()

        order = frame_to_patch()
        for c in range(0, D, COLS):
            block = received[f, :, :, c : c + COLS].astype(F32).reshape(ROWS, COLS).astype(BF)
            x[f, :, c : c + COLS] = dot_nn(order, block).astype(BF)
        frame_rows = pl.ds(pl.multiple_of(f * SEQ, SEQ), SEQ)
        for c in range(0, 3 * D, COLS):
            product = dot_nn(x[f], wtqkv[:, c : c + COLS]).astype(BF).reshape(PATCH, SEQ, COLS)
            if c < 2 * D:
                tqk[:, frame_rows, c : c + COLS] = product
            else:
                tv[:, frame_rows, c - 2 * D : c - 2 * D + COLS] = product
        return 0

    lax.fori_loop(0, LOCAL, temporal_qkv, 0)

    def temporal(p, _):
        frames_all = LOCAL * SEQ
        for c in range(0, D, COLS):
            tvt[c : c + COLS, :] = tv[p, :, c : c + COLS].astype(F32).T
        for head in range(HEADS):
            first, last = window(head)
            keys = tqk[p, :, D + first : D + last] * head_mask(head)
            values_t = tvt[HEAD * head : HEAD * (head + 1), :frames_all].astype(BF)
            tmix_t[HEAD * head : HEAD * (head + 1), :frames_all] = attend_t(tqk[p, :, first:last], keys, values_t)
        for c in range(0, D, COLS):
            block = tmix_t[c : c + COLS, :].T.astype(BF)
            for f in range(LOCAL):
                tmix[f, pl.ds(pl.multiple_of(p * SEQ, SEQ), SEQ), c : c + COLS] = block[f * SEQ : (f + 1) * SEQ]
        return 0

    tv[:, LOCAL * SEQ :, :] = jnp.zeros((PATCH, LANES - LOCAL * SEQ, D), BF)
    tmix_t[...] = jnp.zeros((D, LANES), F32)
    lax.fori_loop(0, PATCH, temporal, 0)

    own_caption.wait()
    pltpu.make_async_copy(cap.at[pl.ds(0, SEQ - 1)], cap.at[pl.ds(0, SEQ - 1)], c_recv).wait()
    swap_copy().wait()
    for head in range(HEADS):
        first, last = window(head)
        place = placed(head)
        keys = dot_nn(cap[head], place).astype(BF)
        values = dot_nn(cap[HEADS + head], place).astype(BF)
        cap_scores[head * SPAN : (head + 1) * SPAN, :] = dot_nt(
            keys, wg[0, :, :, first:last].reshape(D, last - first)
        ).astype(BF)
        rows = wg[1].reshape(D, D)[first:last]
        cap_values[head * SPAN : (head + 1) * SPAN, :] = dot_nn(values, rows).astype(BF)

    loads[6].wait()
    for f in range(LOCAL):
        pltpu.make_async_copy(
            sent.at[f, pl.ds(0, SEQ - 1)], sent.at[f, pl.ds(0, SEQ - 1)], f_send.at[f]
        ).wait()

    def finish(f, _):
        after = modulated
        for c in range(0, D, COLS):
            branch = dot_nn(tmix[f], wtp[:, c : c + COLS])
            after[:, c : c + COLS] = (
                x[f, :, c : c + COLS].astype(F32) + modulation[2:3, c : c + COLS] * branch
            ).astype(BF)
        allowed = lax.broadcasted_iota(jnp.int32, (SPAN, ROWS), 0) < caption_len[0]
        for head in range(HEADS):
            span = slice(head * SPAN, (head + 1) * SPAN)
            scores = jnp.where(allowed, dot_nt(cap_scores[span, :], after[...]), -1e30)
            top = jnp.max(scores, axis=0, keepdims=True)
            weights = jnp.exp2((scores - top) * EXP_SCALE)
            weights = weights * (1.0 / jnp.sum(weights, axis=0, keepdims=True))
            weights_n[:, span] = weights.T.astype(BF)
        order = patch_to_frame()
        for c in range(0, D, COLS):
            branch = dot_nn(weights_n[...], cap_values[:, c : c + COLS])
            rows = (after[:, c : c + COLS].astype(F32) + branch).astype(BF)
            sent[f, :, :, c : c + COLS] = dot_nn(order, rows).reshape(SEQ, PATCH, COLS).astype(BF)

        @pl.loop(1, SEQ)
        def _(k):
            peer = peer_of(k)
            pltpu.make_async_remote_copy(
                sent.at[f, peer], out_ref.at[f, me], r_send.at[f], r_recv.at[f],
                device_id={"seq": peer}, device_id_type=MESH,
            ).start()

        pltpu.make_async_copy(sent.at[f, me], out_ref.at[f, me], local_sem.at[2 + f]).start()
        return 0

    lax.fori_loop(0, LOCAL, finish, 0)

    for f in range(LOCAL):
        pltpu.make_async_copy(sent.at[f, me], out_ref.at[f, me], local_sem.at[2 + f]).wait()
        pltpu.make_async_copy(
            sent.at[f, pl.ds(0, SEQ - 1)], sent.at[f, pl.ds(0, SEQ - 1)], r_send.at[f]
        ).wait()
        pltpu.make_async_copy(
            out_ref.at[f, pl.ds(0, SEQ - 1)], out_ref.at[f, pl.ds(0, SEQ - 1)], r_recv.at[f]
        ).wait()
    pltpu.make_async_copy(wy.at[pl.ds(0, 3)], wy.at[pl.ds(0, 3)], y_send).wait()
    pltpu.make_async_copy(wg.at[core, pl.ds(0, 7)], wg.at[core, pl.ds(0, 7)], g_send).wait()
    pltpu.make_async_copy(cap.at[pl.ds(0, SEQ - 1)], cap.at[pl.ds(0, SEQ - 1)], c_send).wait()


def shards(
    frames_in, modulation, caption_kv, caption_len,
    w_spatial_qkv, w_spatial_proj, w_temporal_qkv, w_temporal_proj, w_cross_q, w_cross_out,
):
    caption = jnp.pad(caption_kv, ((0, SPAN - CAP), (0, LANES - HEAD)))
    crossed = jnp.stack([w_cross_q, w_cross_out])
    vmem = pl.BlockSpec(memory_space=pltpu.VMEM)
    whole = pl.BlockSpec(memory_space=pl.ANY)
    dma = pltpu.SemaphoreType.DMA
    out = pl.pallas_call(
        kernel,
        out_shape=jax.ShapeDtypeStruct((LOCAL, SEQ, PATCH, D), BF),
        in_specs=[pl.BlockSpec(memory_space=pltpu.SMEM), whole, vmem] + [whole] * 6,
        out_specs=whole,
        scratch_shapes=[
            pltpu.VMEM((LOCAL, ROWS, D), BF),
            pltpu.VMEM((D, 3 * D), BF),
            pltpu.VMEM((D, D), BF),
            pltpu.VMEM((D, 3 * D), BF),
            pltpu.VMEM((D, D), BF),
            pltpu.VMEM((4, 36, D), BF),
            pltpu.VMEM((2, 8, 144, D), BF),
            pltpu.VMEM((SEQ, SPAN, LANES), BF),
            pltpu.VMEM((HEADS * SPAN, D), BF),
            pltpu.VMEM((HEADS * SPAN, D), BF),
            pltpu.VMEM((ROWS, D), BF),
            pltpu.VMEM((ROWS, 2 * D), BF),
            pltpu.VMEM((D, ROWS), F32),
            pltpu.VMEM((D, ROWS), F32),
            pltpu.VMEM((ROWS, D), BF),
            pltpu.VMEM((LOCAL, SEQ, PATCH, D), BF),
            pltpu.VMEM((LOCAL, SEQ, PATCH, D), BF),
            pltpu.VMEM((LOCAL, ROWS, D), BF),
            pltpu.VMEM((PATCH, LOCAL * SEQ, 2 * D), BF),
            pltpu.VMEM((PATCH, LANES, D), BF),
            pltpu.VMEM((D, LANES), F32),
            pltpu.VMEM((D, LANES), F32),
            pltpu.VMEM((LOCAL, ROWS, D), BF),
            pltpu.VMEM((ROWS, HEADS * SPAN), BF),
            dma((7,)),
            dma, dma, dma, dma, dma, dma, dma, dma,
            dma((LOCAL,)), dma((LOCAL,)), dma((LOCAL,)), dma((LOCAL,)),
            dma((5,)),
        ],
        compiler_params=pltpu.CompilerParams(
            collective_id=0, has_side_effects=True, vmem_limit_bytes=65 * 1024 * 1024
        ),
        name="block",
    )(
        caption_len, frames_in, modulation, caption,
        w_spatial_qkv, w_spatial_proj, w_temporal_qkv, w_temporal_proj, crossed,
    )
    return out.reshape(frames_in.shape)


def solution(mesh):
    in_specs = (
        P(("dp", "seq"), None, None),
        P("dp", None),
        P("dp", "seq"),
        P("dp"),
        P(),
        P(),
        P(),
        P(),
        P("seq", None),
        P("seq", None),
    )
    out_specs = P(("dp", "seq"), None, None)
    return jax.shard_map(shards, mesh=mesh, in_specs=in_specs, out_specs=out_specs, check_vma=False)
```

```python
import math

import jax
import jax.numpy as jnp
from jax import lax
from jax.experimental import pallas as pl
from jax.experimental.pallas import tpu as pltpu
from jax.sharding import PartitionSpec as P

HEADS = 16
HEAD = 72
D = 1152
LANES = 128
SEQ = 32
LOCAL = 3
PATCH = 8
CAP = 120
ROWS = 256
BF = jnp.bfloat16
F32 = jnp.float32
MESH = pl.DeviceIdType.MESH
EXP_SCALE = HEAD ** (-0.5) * math.log2(math.e)


def window(head):
    low = HEAD * head
    return low // LANES * LANES, -(-(low + HEAD) // LANES) * LANES


def dot_nt(a, b):
    return lax.dot_general(a, b, (((1,), (1,)), ((), ())), preferred_element_type=F32)


def dot_nn(a, b):
    return jnp.dot(a, b, preferred_element_type=F32)


def head_mask(head):
    first, last = window(head)
    lane = lax.broadcasted_iota(jnp.int32, (1, last - first), 1) + first
    return jnp.where((lane >= HEAD * head) & (lane < HEAD * (head + 1)), 1.0, 0.0).astype(BF)


def placed(head):
    first, last = window(head)
    shape = (HEAD, last - first)
    feature = lax.broadcasted_iota(jnp.int32, shape, 0)
    lane = lax.broadcasted_iota(jnp.int32, shape, 1) + first
    return jnp.where(lane == feature + HEAD * head, 1.0, 0.0).astype(BF)


def frame_to_patch():
    row = lax.broadcasted_iota(jnp.int32, (ROWS, ROWS), 0)
    column = lax.broadcasted_iota(jnp.int32, (ROWS, ROWS), 1)
    return jnp.where(column == (row % SEQ) * PATCH + row // SEQ, 1.0, 0.0).astype(BF)


def patch_to_frame():
    row = lax.broadcasted_iota(jnp.int32, (ROWS, ROWS), 0)
    column = lax.broadcasted_iota(jnp.int32, (ROWS, ROWS), 1)
    return jnp.where(column == (row % PATCH) * SEQ + row // PATCH, 1.0, 0.0).astype(BF)


def spans(first, last, step=512):
    return [(c, min(c + step, last)) for c in range(first, last, step)]


def attend_heads(score, value_t, store, buffers, group, allowed=None):
    scores, weights, inverse = buffers
    groups = HEADS // group

    def multiply(g):
        for i in range(group):
            scores[g % 2, i] = score(g * group + i)

    def soften(g):
        for i in range(group):
            rows = scores[g % 2, i]
            if allowed is not None:
                rows = jnp.where(allowed, rows, -1e30)
            top = jnp.max(rows, axis=0, keepdims=True)
            raised = jnp.exp2((rows - top) * EXP_SCALE)
            inverse[g % 2, i] = 1.0 / jnp.sum(raised, axis=0, keepdims=True)
            weights[g % 2, i] = raised.astype(BF)

    def mix(g):
        for i in range(group):
            store(g * group + i, dot_nn(value_t(g * group + i), weights[g % 2, i]) * inverse[g % 2, i])

    multiply(0)
    for g in range(groups):
        if g + 1 < groups:
            multiply(g + 1)
        soften(g)
        mix(g)


def landed(ref, semaphore):
    pltpu.make_async_copy(ref, ref, semaphore).wait()


def kernel(
    caption_len, frames_ref, modulation, caption_ref, wsqkv_ref, wsp_ref, wtqkv_ref, wtp_ref, wcq_ref, wco_ref,
    out_ref,
    frames, wsqkv, wsp, wtqkv, wtp, wy, wg, cap, cap_keys,
    modulated, qk, vt, mix_t, mix, sent, received, x, tqk, tv, tvt, tmix_t, tmix,
    scores, weights, inverse, tscores, tweights, tinverse, cscores, cweights, cinverse,
    load_sem, y_send, y_recv, g_send, g_recv, z_send, z_recv, s_send, s_recv, c_send, c_recv,
    f_send, f_recv, r_send, r_recv, local_sem,
):
    me = lax.axis_index("seq")
    dp = lax.axis_index("dp")
    core = dp % 2
    my_x, my_z, my_y = me // 8, (me // 4) % 2, me % 4
    other_core = dp + 1 - 2 * core
    across = (dp + 2) % 4

    def peer_of(k):
        y = (my_y + k % 4) % 4
        x_ = (my_x + (k // 4) % 4) % 4
        z = (my_z + k // 16) % 2
        return x_ * 8 + z * 4 + y

    facing = my_x * 8 + (1 - my_z) * 4 + my_y

    barrier = pltpu.get_barrier_semaphore()

    @pl.loop(1, SEQ)
    def _(k):
        pl.semaphore_signal(barrier, inc=1, device_id={"seq": peer_of(k)}, device_id_type=MESH)

    pl.semaphore_signal(barrier, inc=1, device_id={"dp": other_core}, device_id_type=MESH)
    pl.semaphore_signal(barrier, inc=1, device_id={"dp": across, "seq": facing}, device_id_type=MESH)

    def load(i):
        source, target = [
            (frames_ref.at[0], frames.at[0]),
            (wsqkv_ref.at[:, :1024], wsqkv.at[:, :1024]),
            (wsqkv_ref.at[:, 1024 : 2 * D], wsqkv.at[:, 1024 : 2 * D]),
            (wsqkv_ref.at[:, 2 * D :], wsqkv.at[:, 2 * D :]),
            (wsp_ref, wsp),
            (frames_ref.at[pl.ds(1, 2)], frames.at[pl.ds(1, 2)]),
            (wtqkv_ref, wtqkv),
            (wtp_ref, wtp),
        ][i]
        return pltpu.make_async_copy(source, target, load_sem.at[i])

    for i in range(3):
        load(i).start()
    own_caption = pltpu.make_async_copy(caption_ref, cap.at[me], local_sem.at[0])
    own_caption.start()

    def own_weight(source):
        return pltpu.make_async_copy(source, wy.at[my_x * 4 + my_y], local_sem.at[1])

    def first_gather(source):
        own_weight(source).start()

        @pl.loop(1, 4)
        def _(k):
            peer = (my_x + core * k) % 4 * 8 + my_z * 4 + (my_y + (1 - core) * k) % 4
            pltpu.make_async_remote_copy(
                source, wy.at[my_x * 4 + my_y], y_send, y_recv, device_id={"seq": peer}, device_id_type=MESH
            ).start()

    def second_gather():
        own_weight(wcq_ref).wait()
        landed(wy.at[pl.ds(0, 3)], y_recv)

        @pl.loop(0, 12)
        def _(n):
            k, i = 1 + n // 4, n % 4
            slot = (1 - core) * (my_x * 4 + i) + core * (i * 4 + my_y)
            peer = (my_x + (1 - core) * k) % 4 * 8 + my_z * 4 + (my_y + core * k) % 4
            pltpu.make_async_remote_copy(
                wy.at[slot], wy.at[slot], g_send, g_recv, device_id={"seq": peer}, device_id_type=MESH
            ).start()

    def third_gather():
        landed(wy.at[pl.ds(0, 12)], g_recv)
        for group in range(4):
            for first, last in spans(0, D):
                total = None
                for y in range(4):
                    row = lax.broadcasted_iota(jnp.int32, (144, 36), 0)
                    column = lax.broadcasted_iota(jnp.int32, (144, 36), 1)
                    place = jnp.where(row == column + 36 * y, 1.0, 0.0).astype(BF)
                    term = dot_nn(place, wy[group * 4 + y, :, first:last])
                    total = term if total is None else total + term
                wg[core, group * 2 + my_z, :, first:last] = total.astype(BF)
        for group in range(4):
            block = wg.at[core, group * 2 + my_z]
            pltpu.make_async_remote_copy(
                block, block, z_send, z_recv,
                device_id={"dp": dp if group == 0 else across, "seq": facing}, device_id_type=MESH,
            ).start()
            swap(group * 2 + my_z, 0).start()

    def swap(block, half):
        return pltpu.make_async_remote_copy(
            wg.at[core, block], wg.at[core, block], s_send.at[half], s_recv.at[half],
            device_id={"dp": other_core}, device_id_type=MESH,
        )

    def last_gather():
        landed(wg.at[core, pl.ds(0, 4)], z_recv)
        for group in range(4):
            swap(group * 2 + 1 - my_z, 1).start()

    def spatial(f, _):
        @pl.when(f == 0)
        def _():
            load(0).wait()

        @pl.when(f == 1)
        def _():
            load(5).wait()

        @pl.loop(0, ROWS // 32, unroll=4)
        def _(r):
            rows = pl.ds(pl.multiple_of(r * 32, 32), 32)
            wide = frames[f, rows, :].astype(F32)
            centered = wide - jnp.mean(wide, axis=-1, keepdims=True)
            variance = jnp.mean(centered * centered, axis=-1, keepdims=True)
            normed = centered * lax.rsqrt(variance + 1e-06)
            modulated[rows, :] = (normed * (1.0 + modulation[1:2, :]) + modulation[0:1, :]).astype(BF)

        @pl.when(f == 0)
        def _():
            pl.semaphore_wait(barrier, SEQ + 1)

            @pl.when(core == 0)
            def _():
                first_gather(wcq_ref)

            @pl.when(core == 1)
            def _():
                first_gather(wco_ref)

            load(1).wait()
            load(3).start()
            load(4).start()

        for first, last in spans(0, 1024):
            qk[:, first:last] = dot_nn(modulated[...], wsqkv[:, first:last]).astype(BF)

        @pl.when(f == 0)
        def _():
            load(2).wait()
            load(5).start()

        for first, last in spans(1024, 2 * D):
            qk[:, first:last] = dot_nn(modulated[...], wsqkv[:, first:last]).astype(BF)

        @pl.when(f == 0)
        def _():
            load(3).wait()
            load(6).start()
            second_gather()

            @pl.loop(1, SEQ)
            def _(k):
                pltpu.make_async_remote_copy(
                    caption_ref, cap.at[me], c_send, c_recv, device_id={"seq": peer_of(k)}, device_id_type=MESH
                ).start()

        for first, last in spans(0, D):
            vt[first:last, :] = dot_nn(modulated[...], wsqkv[:, 2 * D + first : 2 * D + last]).T

        @pl.when(f == 1)
        def _():
            third_gather()

        def score(head):
            first, last = window(head)
            return dot_nt(qk[:, D + first : D + last] * head_mask(head), qk[:, first:last])

        def store(head, rows):
            mix_t[HEAD * head : HEAD * (head + 1), :] = rows

        attend_heads(
            score, lambda head: vt[HEAD * head : HEAD * (head + 1), :].astype(BF), store, (scores, weights, inverse), 4
        )
        for first, last in spans(0, D):
            mix[:, first:last] = mix_t[first:last, :].T.astype(BF)

        @pl.when(f == 0)
        def _():
            load(4).wait()
            load(7).start()

        for first, last in spans(0, D):
            branch = dot_nn(mix[...], wsp[:, first:last])
            after = frames[f, :, first:last].astype(F32) + modulation[2:3, first:last] * branch
            sent[f, :, :, first:last] = after.reshape(SEQ, PATCH, last - first).astype(BF)

        @pl.loop(1, SEQ)
        def _(k):
            peer = peer_of(k)
            pltpu.make_async_remote_copy(
                sent.at[f, peer], received.at[f, me], f_send.at[f], f_recv.at[f],
                device_id={"seq": peer}, device_id_type=MESH,
            ).start()

        received[f, me] = sent[f, me]
        return 0

    lax.fori_loop(0, LOCAL, spatial, 0)

    def temporal_qkv(f, _):
        landed(received.at[f, pl.ds(0, SEQ - 1)], f_recv.at[f])

        @pl.when(f == 0)
        def _():
            load(6).wait()

        order = frame_to_patch()
        for first, last in spans(0, D):
            block = received[f, :, :, first:last].astype(F32).reshape(ROWS, last - first).astype(BF)
            x[f, :, first:last] = dot_nn(order, block).astype(BF)
        frame_rows = pl.ds(pl.multiple_of(f * SEQ, SEQ), SEQ)
        for first, last in spans(0, 2 * D):
            product = dot_nn(x[f], wtqkv[:, first:last]).astype(BF)
            tqk[:, frame_rows, first:last] = product.reshape(PATCH, SEQ, last - first)
        for first, last in spans(0, D):
            product = dot_nn(x[f], wtqkv[:, 2 * D + first : 2 * D + last]).astype(BF)
            tv[:, frame_rows, first:last] = product.reshape(PATCH, SEQ, last - first)

        @pl.when(f == 0)
        def _():
            own_caption.wait()
            landed(cap.at[pl.ds(0, SEQ - 1)], c_recv)
            for head in range(HEADS):
                first, last = window(head)
                cap_keys[head, :, : last - first] = lax.dot_general(
                    cap[head], placed(head), (((0,), (0,)), ((), ())), preferred_element_type=F32
                ).astype(BF)

        return 0

    lax.fori_loop(0, LOCAL, temporal_qkv, 0)

    frames_all = LOCAL * SEQ

    def temporal(p, _):
        for first, last in spans(0, D, 384):
            tvt[first:last, :] = tv[p, :, first:last].astype(F32).T

        def score(head):
            first, last = window(head)
            return dot_nt(tqk[p, :, D + first : D + last] * head_mask(head), tqk[p, :, first:last])

        def store(head, rows):
            tmix_t[HEAD * head : HEAD * (head + 1), :frames_all] = rows

        attend_heads(
            score, lambda head: tvt[HEAD * head : HEAD * (head + 1), :frames_all].astype(BF), store,
            (tscores, tweights, tinverse), 8,
        )
        for first, last in spans(0, D, 384):
            block = tmix_t[first:last, :].T.astype(BF)
            for f in range(LOCAL):
                tmix[f, pl.ds(pl.multiple_of(p * SEQ, SEQ), SEQ), first:last] = block[f * SEQ : (f + 1) * SEQ]

        @pl.when(p == 2)
        def _():
            last_gather()

        return 0

    tv[:, frames_all:, :] = jnp.zeros((PATCH, LANES - frames_all, D), BF)
    tmix_t[...] = jnp.zeros((D, LANES), F32)
    lax.fori_loop(0, PATCH, temporal, 0)

    load(7).wait()
    for f in range(LOCAL):
        landed(sent.at[f, pl.ds(0, SEQ - 1)], f_send.at[f])

    def finish(f, _):
        after = modulated
        for first, last in spans(0, D):
            branch = dot_nn(tmix[f], wtp[:, first:last])
            after[:, first:last] = (
                x[f, :, first:last].astype(F32) + modulation[2:3, first:last] * branch
            ).astype(BF)

        @pl.when(f == 0)
        def _():
            for half in range(2):
                landed(wg.at[core, pl.ds(0, 4)], s_recv.at[half])

        for first, last in spans(0, D):
            qk[:, first:last] = dot_nn(after[...], wg[0, :, :, first:last].reshape(D, last - first)).astype(BF)

        def score(head):
            first, last = window(head)
            return dot_nt(cap_keys[head, :, : last - first], qk[:, first:last])

        def store(head, rows):
            mix_t[HEAD * head : HEAD * (head + 1), :] = rows

        allowed = lax.broadcasted_iota(jnp.int32, (CAP, ROWS), 0) < caption_len[0]
        attend_heads(score, lambda head: cap[HEADS + head], store, (cscores, cweights, cinverse), 4, allowed)
        for first, last in spans(0, D):
            mix[:, first:last] = mix_t[first:last, :].T.astype(BF)
        order = patch_to_frame()
        for first, last in spans(0, D):
            branch = dot_nn(mix[...], wg[1, :, :, first:last].reshape(D, last - first))
            rows = (after[:, first:last].astype(F32) + branch).astype(BF)
            sent[f, :, :, first:last] = dot_nn(order, rows).reshape(SEQ, PATCH, last - first).astype(BF)

        @pl.loop(1, SEQ)
        def _(k):
            peer = peer_of(k)
            pltpu.make_async_remote_copy(
                sent.at[f, peer], out_ref.at[f, me], r_send.at[f], r_recv.at[f],
                device_id={"seq": peer}, device_id_type=MESH,
            ).start()

        pltpu.make_async_copy(sent.at[f, me], out_ref.at[f, me], local_sem.at[2 + f]).start()
        return 0

    lax.fori_loop(0, LOCAL, finish, 0)

    for f in range(LOCAL):
        pltpu.make_async_copy(sent.at[f, me], out_ref.at[f, me], local_sem.at[2 + f]).wait()
        landed(sent.at[f, pl.ds(0, SEQ - 1)], r_send.at[f])
        landed(out_ref.at[f, pl.ds(0, SEQ - 1)], r_recv.at[f])
    landed(wy.at[pl.ds(0, 3)], y_send)
    landed(wy.at[pl.ds(0, 12)], g_send)
    landed(wg.at[core, pl.ds(0, 4)], z_send)
    for half in range(2):
        landed(wg.at[core, pl.ds(0, 4)], s_send.at[half])
    landed(cap.at[pl.ds(0, SEQ - 1)], c_send)


def shards(
    frames_in, modulation, caption_kv, caption_len,
    w_spatial_qkv, w_spatial_proj, w_temporal_qkv, w_temporal_proj, w_cross_q, w_cross_out,
):
    vmem = pl.BlockSpec(memory_space=pltpu.VMEM)
    whole = pl.BlockSpec(memory_space=pl.ANY)
    dma = pltpu.SemaphoreType.DMA
    out = pl.pallas_call(
        kernel,
        out_shape=jax.ShapeDtypeStruct((LOCAL, SEQ, PATCH, D), BF),
        in_specs=[pl.BlockSpec(memory_space=pltpu.SMEM), whole, vmem] + [whole] * 7,
        out_specs=whole,
        scratch_shapes=[
            pltpu.VMEM((LOCAL, ROWS, D), BF),
            pltpu.VMEM((D, 3 * D), BF),
            pltpu.VMEM((D, D), BF),
            pltpu.VMEM((D, 3 * D), BF),
            pltpu.VMEM((D, D), BF),
            pltpu.VMEM((16, 36, D), BF),
            pltpu.VMEM((2, 8, 144, D), BF),
            pltpu.VMEM((SEQ, HEAD, CAP), BF),
            pltpu.VMEM((HEADS, CAP, 2 * LANES), BF),
            pltpu.VMEM((ROWS, D), BF),
            pltpu.VMEM((ROWS, 2 * D), BF),
            pltpu.VMEM((D, ROWS), F32),
            pltpu.VMEM((D, ROWS), F32),
            pltpu.VMEM((ROWS, D), BF),
            pltpu.VMEM((LOCAL, SEQ, PATCH, D), BF),
            pltpu.VMEM((LOCAL, SEQ, PATCH, D), BF),
            pltpu.VMEM((LOCAL, ROWS, D), BF),
            pltpu.VMEM((PATCH, LOCAL * SEQ, 2 * D), BF),
            pltpu.VMEM((PATCH, LANES, D), BF),
            pltpu.VMEM((D, LANES), F32),
            pltpu.VMEM((D, LANES), F32),
            pltpu.VMEM((LOCAL, ROWS, D), BF),
            pltpu.VMEM((2, 4, ROWS, ROWS), F32),
            pltpu.VMEM((2, 4, ROWS, ROWS), BF),
            pltpu.VMEM((2, 4, 1, ROWS), F32),
            pltpu.VMEM((2, 8, LOCAL * SEQ, LOCAL * SEQ), F32),
            pltpu.VMEM((2, 8, LOCAL * SEQ, LOCAL * SEQ), BF),
            pltpu.VMEM((2, 8, 1, LOCAL * SEQ), F32),
            pltpu.VMEM((2, 4, CAP, ROWS), F32),
            pltpu.VMEM((2, 4, CAP, ROWS), BF),
            pltpu.VMEM((2, 4, 1, ROWS), F32),
            dma((8,)),
            dma, dma, dma, dma, dma, dma, dma((2,)), dma((2,)), dma, dma,
            dma((LOCAL,)), dma((LOCAL,)), dma((LOCAL,)), dma((LOCAL,)),
            dma((5,)),
        ],
        compiler_params=pltpu.CompilerParams(
            collective_id=0, has_side_effects=True, vmem_limit_bytes=64 * 1024 * 1024
        ),
        name="block",
    )(
        caption_len, frames_in, modulation, caption_kv.T,
        w_spatial_qkv, w_spatial_proj, w_temporal_qkv, w_temporal_proj, w_cross_q, w_cross_out,
    )
    return out.reshape(frames_in.shape)


def solution(mesh):
    in_specs = (
        P(("dp", "seq"), None, None),
        P("dp", None),
        P("dp", "seq"),
        P("dp"),
        P(),
        P(),
        P(),
        P(),
        P("seq", None),
        P("seq", None),
    )
    out_specs = P(("dp", "seq"), None, None)
    return jax.shard_map(shards, mesh=mesh, in_specs=in_specs, out_specs=out_specs, check_vma=False)
```

```python
import math

import jax
import jax.numpy as jnp
from jax import lax
from jax.experimental import pallas as pl
from jax.experimental.pallas import tpu as pltpu
from jax.sharding import PartitionSpec as P

HEADS = 16
HEAD = 72
D = 1152
LANES = 128
SEQ = 32
LOCAL = 3
PATCH = 8
CAP = 120
ROWS = 256
HALVES = ((0, 640), (640, D))
BF = jnp.bfloat16
F32 = jnp.float32
MESH = pl.DeviceIdType.MESH
EXP_SCALE = HEAD ** (-0.5) * math.log2(math.e)


def window(head):
    low = HEAD * head
    return low // LANES * LANES, -(-(low + HEAD) // LANES) * LANES


def dot_nt(a, b):
    return lax.dot_general(a, b, (((1,), (1,)), ((), ())), preferred_element_type=F32)


def dot_nn(a, b):
    return jnp.dot(a, b, preferred_element_type=F32)


def head_mask(head):
    first, last = window(head)
    lane = lax.broadcasted_iota(jnp.int32, (1, last - first), 1) + first
    return jnp.where((lane >= HEAD * head) & (lane < HEAD * (head + 1)), 1.0, 0.0).astype(BF)


def placed(head):
    first, last = window(head)
    shape = (HEAD, last - first)
    feature = lax.broadcasted_iota(jnp.int32, shape, 0)
    lane = lax.broadcasted_iota(jnp.int32, shape, 1) + first
    return jnp.where(lane == feature + HEAD * head, 1.0, 0.0).astype(BF)


def frame_to_patch():
    row = lax.broadcasted_iota(jnp.int32, (ROWS, ROWS), 0)
    column = lax.broadcasted_iota(jnp.int32, (ROWS, ROWS), 1)
    return jnp.where(column == (row % SEQ) * PATCH + row // SEQ, 1.0, 0.0).astype(BF)


def patch_to_frame():
    row = lax.broadcasted_iota(jnp.int32, (ROWS, ROWS), 0)
    column = lax.broadcasted_iota(jnp.int32, (ROWS, ROWS), 1)
    return jnp.where(column == (row % PATCH) * SEQ + row // PATCH, 1.0, 0.0).astype(BF)


def spans(first, last, step=512):
    return [(c, min(c + step, last)) for c in range(first, last, step)]


def attend_heads(score, value_t, store, buffers, group, allowed=None):
    scores, weights, inverse = buffers
    groups = HEADS // group

    def multiply(g):
        for i in range(group):
            scores[g % 2, i] = score(g * group + i)

    def soften(g):
        for i in range(group):
            rows = scores[g % 2, i]
            if allowed is not None:
                rows = jnp.where(allowed, rows, -1e30)
            top = jnp.max(rows, axis=0, keepdims=True)
            raised = jnp.exp2((rows - top) * EXP_SCALE)
            inverse[g % 2, i] = 1.0 / jnp.sum(raised, axis=0, keepdims=True)
            weights[g % 2, i] = raised.astype(BF)

    def mix(g):
        for i in range(group):
            store(g * group + i, dot_nn(value_t(g * group + i), weights[g % 2, i]) * inverse[g % 2, i])

    multiply(0)
    for g in range(groups):
        if g + 1 < groups:
            multiply(g + 1)
        soften(g)
        mix(g)


def landed(ref, semaphore):
    pltpu.make_async_copy(ref, ref, semaphore).wait()


def kernel(
    caption_len, frames_ref, modulation, caption_ref, wsqkv_ref, wsp_ref, wtqkv_ref, wtp_ref, wcq_ref, wco_ref,
    out_ref,
    frames, wsqkv, wsp, wtqkv, wtp, wy, wg, cap, cap_keys,
    modulated, qk, vt, mix_t, mix, sent, received, x, tqk, tv, tvt, tmix_t, tmix,
    scores, weights, inverse, tscores, tweights, tinverse, cscores, cweights, cinverse,
    load_sem, y_send, y_recv, g_send, g_recv, z_send, z_recv, s_send, s_recv, c_send, c_recv,
    f_send, f_recv, r_send, r_recv, local_sem,
):
    me = lax.axis_index("seq")
    dp = lax.axis_index("dp")
    core = dp % 2
    my_x, my_z, my_y = me // 8, (me // 4) % 2, me % 4
    other_core = dp + 1 - 2 * core
    across = (dp + 2) % 4

    def peer_of(k):
        y = (my_y + k % 4) % 4
        x_ = (my_x + (k // 4) % 4) % 4
        z = (my_z + k // 16) % 2
        return x_ * 8 + z * 4 + y

    facing = my_x * 8 + (1 - my_z) * 4 + my_y

    barrier = pltpu.get_barrier_semaphore()

    @pl.loop(1, SEQ)
    def _(k):
        pl.semaphore_signal(barrier, inc=1, device_id={"seq": peer_of(k)}, device_id_type=MESH)

    pl.semaphore_signal(barrier, inc=1, device_id={"dp": other_core}, device_id_type=MESH)
    pl.semaphore_signal(barrier, inc=1, device_id={"dp": across, "seq": facing}, device_id_type=MESH)

    def load(i):
        source, target = [
            (frames_ref.at[0], frames.at[0]),
            (wsqkv_ref.at[:, :1024], wsqkv.at[:, :1024]),
            (wsqkv_ref.at[:, 1024 : 2 * D], wsqkv.at[:, 1024 : 2 * D]),
            (wsqkv_ref.at[:, 2 * D :], wsqkv.at[:, 2 * D :]),
            (wsp_ref, wsp),
            (frames_ref.at[pl.ds(1, 2)], frames.at[pl.ds(1, 2)]),
            (wtqkv_ref, wtqkv),
            (wtp_ref, wtp),
        ][i]
        return pltpu.make_async_copy(source, target, load_sem.at[i])

    for i in range(3):
        load(i).start()
    own_caption = pltpu.make_async_copy(caption_ref, cap.at[me], local_sem.at[0])
    own_caption.start()

    def by_core(step):
        for c in range(2):
            @pl.when(core == c)
            def _():
                step(c, slice(*HALVES[c]))

    def own_weight(m, columns):
        source = (wcq_ref, wco_ref)[m].at[:, columns]
        return pltpu.make_async_copy(source, wy.at[m, my_x * 4 + my_y, :, columns], local_sem.at[5 + m])

    def first_gather(c, columns):
        for m in range(2):
            own_weight(m, columns).start()

        for m, source in enumerate((wcq_ref, wco_ref)):
            @pl.loop(1, 4)
            def _(k):
                peer = (my_x + c * k) % 4 * 8 + my_z * 4 + (my_y + (1 - c) * k) % 4
                pltpu.make_async_remote_copy(
                    source.at[:, columns], wy.at[m, my_x * 4 + my_y, :, columns], y_send.at[m], y_recv.at[m],
                    device_id={"seq": peer}, device_id_type=MESH,
                ).start()

    def second_gather(m):
        def step(c, columns):
            own_weight(m, columns).wait()
            landed(wy.at[m, pl.ds(0, 3), :, columns], y_recv.at[m])

            @pl.loop(0, 12)
            def _(n):
                k, i = 1 + n // 4, n % 4
                block = wy.at[m, my_x * 4 + i if c == 0 else i * 4 + my_y, :, columns]
                peer = (my_x + (1 - c) * k) % 4 * 8 + my_z * 4 + (my_y + c * k) % 4
                pltpu.make_async_remote_copy(
                    block, block, g_send.at[m], g_recv.at[m], device_id={"seq": peer}, device_id_type=MESH
                ).start()

        by_core(step)

    def swap(m, block, half, columns):
        part = wg.at[m, block, :, columns]
        return pltpu.make_async_remote_copy(
            part, part, s_send.at[m, half], s_recv.at[m, half], device_id={"dp": other_core}, device_id_type=MESH
        )

    def third_gather(m):
        def step(c, columns):
            landed(wy.at[m, pl.ds(0, 12), :, columns], g_recv.at[m])
            for group in range(4):
                total = None
                for y in range(4):
                    row = lax.broadcasted_iota(jnp.int32, (144, 36), 0)
                    column = lax.broadcasted_iota(jnp.int32, (144, 36), 1)
                    place = jnp.where(row == column + 36 * y, 1.0, 0.0).astype(BF)
                    term = dot_nn(place, wy[m, group * 4 + y, :, columns])
                    total = term if total is None else total + term
                wg[m, group * 2 + my_z, :, columns] = total.astype(BF)
            for group in range(4):
                block = wg.at[m, group * 2 + my_z, :, columns]
                pltpu.make_async_remote_copy(
                    block, block, z_send.at[m], z_recv.at[m],
                    device_id={"dp": dp if group < 2 * m else across, "seq": facing}, device_id_type=MESH,
                ).start()
                swap(m, group * 2 + my_z, 0, columns).start()

        by_core(step)

    def last_gather(m):
        def step(c, columns):
            landed(wg.at[m, pl.ds(0, 4), :, columns], z_recv.at[m])
            for group in range(4):
                swap(m, group * 2 + 1 - my_z, 1, columns).start()

        by_core(step)

    def whole_weight(m):
        def step(c, columns):
            for half in range(2):
                landed(wg.at[m, pl.ds(0, 4), :, slice(*HALVES[1 - c])], s_recv.at[m, half])

        by_core(step)

    def sent_weights(c, columns):
        for m in range(2):
            landed(wy.at[m, pl.ds(0, 3), :, columns], y_send.at[m])
            landed(wy.at[m, pl.ds(0, 12), :, columns], g_send.at[m])
            landed(wg.at[m, pl.ds(0, 4), :, columns], z_send.at[m])
            for half in range(2):
                landed(wg.at[m, pl.ds(0, 4), :, columns], s_send.at[m, half])

    pl.semaphore_wait(barrier, SEQ + 1)

    by_core(first_gather)

    def spatial(f, _):
        @pl.when(f == 0)
        def _():
            load(0).wait()

        @pl.when(f == 1)
        def _():
            load(5).wait()

        @pl.loop(0, ROWS // 32, unroll=4)
        def _(r):
            rows = pl.ds(pl.multiple_of(r * 32, 32), 32)
            wide = frames[f, rows, :].astype(F32)
            centered = wide - jnp.mean(wide, axis=-1, keepdims=True)
            variance = jnp.mean(centered * centered, axis=-1, keepdims=True)
            normed = centered * lax.rsqrt(variance + 1e-06)
            modulated[rows, :] = (normed * (1.0 + modulation[1:2, :]) + modulation[0:1, :]).astype(BF)

        @pl.when(f == 0)
        def _():
            load(1).wait()
            load(3).start()
            load(4).start()

        for first, last in spans(0, 1024):
            qk[:, first:last] = dot_nn(modulated[...], wsqkv[:, first:last]).astype(BF)

        @pl.when(f == 0)
        def _():
            load(2).wait()
            load(5).start()
            second_gather(0)

        for first, last in spans(1024, 2 * D):
            qk[:, first:last] = dot_nn(modulated[...], wsqkv[:, first:last]).astype(BF)

        @pl.when(f == 0)
        def _():
            load(3).wait()
            load(6).start()

        for first, last in spans(0, D):
            vt[first:last, :] = dot_nn(modulated[...], wsqkv[:, 2 * D + first : 2 * D + last]).T

        def score(head):
            first, last = window(head)
            return dot_nt(qk[:, D + first : D + last] * head_mask(head), qk[:, first:last])

        def store(head, rows):
            mix_t[HEAD * head : HEAD * (head + 1), :] = rows

        attend_heads(
            score, lambda head: vt[HEAD * head : HEAD * (head + 1), :].astype(BF), store, (scores, weights, inverse), 4
        )
        for first, last in spans(0, D):
            mix[:, first:last] = mix_t[first:last, :].T.astype(BF)

        @pl.when(f == 1)
        def _():
            third_gather(0)

        @pl.when(f == 0)
        def _():
            load(4).wait()
            load(7).start()

        for first, last in spans(0, D):
            branch = dot_nn(mix[...], wsp[:, first:last])
            after = frames[f, :, first:last].astype(F32) + modulation[2:3, first:last] * branch
            sent[f, :, :, first:last] = after.reshape(SEQ, PATCH, last - first).astype(BF)

        @pl.loop(1, SEQ)
        def _(k):
            peer = peer_of(k)
            pltpu.make_async_remote_copy(
                sent.at[f, peer], received.at[f, me], f_send.at[f], f_recv.at[f],
                device_id={"seq": peer}, device_id_type=MESH,
            ).start()

        received[f, me] = sent[f, me]
        return 0

    lax.fori_loop(0, LOCAL, spatial, 0)
    second_gather(1)

    @pl.loop(1, SEQ)
    def _(k):
        pltpu.make_async_remote_copy(
            caption_ref, cap.at[me], c_send, c_recv, device_id={"seq": peer_of(k)}, device_id_type=MESH
        ).start()

    def temporal_qkv(f, _):
        landed(received.at[f, pl.ds(0, SEQ - 1)], f_recv.at[f])

        @pl.when(f == 0)
        def _():
            load(6).wait()

        order = frame_to_patch()
        for first, last in spans(0, D):
            block = received[f, :, :, first:last].astype(F32).reshape(ROWS, last - first).astype(BF)
            x[f, :, first:last] = dot_nn(order, block).astype(BF)
        frame_rows = pl.ds(pl.multiple_of(f * SEQ, SEQ), SEQ)
        for first, last in spans(0, 2 * D):
            product = dot_nn(x[f], wtqkv[:, first:last]).astype(BF)
            tqk[:, frame_rows, first:last] = product.reshape(PATCH, SEQ, last - first)
        for first, last in spans(0, D):
            product = dot_nn(x[f], wtqkv[:, 2 * D + first : 2 * D + last]).astype(BF)
            tv[:, frame_rows, first:last] = product.reshape(PATCH, SEQ, last - first)

        return 0

    lax.fori_loop(0, LOCAL, temporal_qkv, 0)
    last_gather(0)

    frames_all = LOCAL * SEQ

    def temporal(p, _):
        for first, last in spans(0, D, 384):
            tvt[first:last, :] = tv[p, :, first:last].astype(F32).T

        def score(head):
            first, last = window(head)
            return dot_nt(tqk[p, :, D + first : D + last] * head_mask(head), tqk[p, :, first:last])

        def store(head, rows):
            tmix_t[HEAD * head : HEAD * (head + 1), :frames_all] = rows

        attend_heads(
            score, lambda head: tvt[HEAD * head : HEAD * (head + 1), :frames_all].astype(BF), store,
            (tscores, tweights, tinverse), 8,
        )
        for first, last in spans(0, D, 384):
            block = tmix_t[first:last, :].T.astype(BF)
            for f in range(LOCAL):
                tmix[f, pl.ds(pl.multiple_of(p * SEQ, SEQ), SEQ), first:last] = block[f * SEQ : (f + 1) * SEQ]

        @pl.when(p == 4)
        def _():
            own_caption.wait()
            landed(cap.at[pl.ds(0, SEQ - 1)], c_recv)
            for head in range(HEADS):
                first, last = window(head)
                cap_keys[head, :, : last - first] = lax.dot_general(
                    cap[head], placed(head), (((0,), (0,)), ((), ())), preferred_element_type=F32
                ).astype(BF)

        @pl.when(p == 5)
        def _():
            third_gather(1)

        return 0

    tv[:, frames_all:, :] = jnp.zeros((PATCH, LANES - frames_all, D), BF)
    tmix_t[...] = jnp.zeros((D, LANES), F32)
    lax.fori_loop(0, PATCH, temporal, 0)

    load(7).wait()
    for f in range(LOCAL):
        landed(sent.at[f, pl.ds(0, SEQ - 1)], f_send.at[f])

    def finish(f, _):
        after = modulated
        for first, last in spans(0, D):
            branch = dot_nn(tmix[f], wtp[:, first:last])
            after[:, first:last] = (
                x[f, :, first:last].astype(F32) + modulation[2:3, first:last] * branch
            ).astype(BF)

        @pl.when(f == 0)
        def _():
            whole_weight(0)
            last_gather(1)

        for first, last in spans(0, D):
            qk[:, first:last] = dot_nn(after[...], wg[0, :, :, first:last].reshape(D, last - first)).astype(BF)

        def score(head):
            first, last = window(head)
            return dot_nt(cap_keys[head, :, : last - first], qk[:, first:last])

        def store(head, rows):
            mix_t[HEAD * head : HEAD * (head + 1), :] = rows

        allowed = lax.broadcasted_iota(jnp.int32, (CAP, ROWS), 0) < caption_len[0]
        attend_heads(score, lambda head: cap[HEADS + head], store, (cscores, cweights, cinverse), 4, allowed)
        for first, last in spans(0, D):
            mix[:, first:last] = mix_t[first:last, :].T.astype(BF)

        @pl.when(f == 0)
        def _():
            whole_weight(1)

        order = patch_to_frame()
        for first, last in spans(0, D):
            branch = dot_nn(mix[...], wg[1, :, :, first:last].reshape(D, last - first))
            rows = (after[:, first:last].astype(F32) + branch).astype(BF)
            sent[f, :, :, first:last] = dot_nn(order, rows).reshape(SEQ, PATCH, last - first).astype(BF)

        @pl.loop(1, SEQ)
        def _(k):
            peer = peer_of(k)
            pltpu.make_async_remote_copy(
                sent.at[f, peer], out_ref.at[f, me], r_send.at[f], r_recv.at[f],
                device_id={"seq": peer}, device_id_type=MESH,
            ).start()

        pltpu.make_async_copy(sent.at[f, me], out_ref.at[f, me], local_sem.at[2 + f]).start()
        return 0

    lax.fori_loop(0, LOCAL, finish, 0)

    for f in range(LOCAL):
        pltpu.make_async_copy(sent.at[f, me], out_ref.at[f, me], local_sem.at[2 + f]).wait()
        landed(sent.at[f, pl.ds(0, SEQ - 1)], r_send.at[f])
        landed(out_ref.at[f, pl.ds(0, SEQ - 1)], r_recv.at[f])
    by_core(sent_weights)
    landed(cap.at[pl.ds(0, SEQ - 1)], c_send)


def shards(
    frames_in, modulation, caption_kv, caption_len,
    w_spatial_qkv, w_spatial_proj, w_temporal_qkv, w_temporal_proj, w_cross_q, w_cross_out,
):
    vmem = pl.BlockSpec(memory_space=pltpu.VMEM)
    whole = pl.BlockSpec(memory_space=pl.ANY)
    dma = pltpu.SemaphoreType.DMA
    out = pl.pallas_call(
        kernel,
        out_shape=jax.ShapeDtypeStruct((LOCAL, SEQ, PATCH, D), BF),
        in_specs=[pl.BlockSpec(memory_space=pltpu.SMEM), whole, vmem] + [whole] * 7,
        out_specs=whole,
        scratch_shapes=[
            pltpu.VMEM((LOCAL, ROWS, D), BF),
            pltpu.VMEM((D, 3 * D), BF),
            pltpu.VMEM((D, D), BF),
            pltpu.VMEM((D, 3 * D), BF),
            pltpu.VMEM((D, D), BF),
            pltpu.VMEM((2, 16, 36, D), BF),
            pltpu.VMEM((2, 8, 144, D), BF),
            pltpu.VMEM((SEQ, HEAD, CAP), BF),
            pltpu.VMEM((HEADS, CAP, 2 * LANES), BF),
            pltpu.VMEM((ROWS, D), BF),
            pltpu.VMEM((ROWS, 2 * D), BF),
            pltpu.VMEM((D, ROWS), F32),
            pltpu.VMEM((D, ROWS), F32),
            pltpu.VMEM((ROWS, D), BF),
            pltpu.VMEM((LOCAL, SEQ, PATCH, D), BF),
            pltpu.VMEM((LOCAL, SEQ, PATCH, D), BF),
            pltpu.VMEM((LOCAL, ROWS, D), BF),
            pltpu.VMEM((PATCH, LOCAL * SEQ, 2 * D), BF),
            pltpu.VMEM((PATCH, LANES, D), BF),
            pltpu.VMEM((D, LANES), F32),
            pltpu.VMEM((D, LANES), F32),
            pltpu.VMEM((LOCAL, ROWS, D), BF),
            pltpu.VMEM((2, 4, ROWS, ROWS), F32),
            pltpu.VMEM((2, 4, ROWS, ROWS), BF),
            pltpu.VMEM((2, 4, 1, ROWS), F32),
            pltpu.VMEM((2, 8, LOCAL * SEQ, LOCAL * SEQ), F32),
            pltpu.VMEM((2, 8, LOCAL * SEQ, LOCAL * SEQ), BF),
            pltpu.VMEM((2, 8, 1, LOCAL * SEQ), F32),
            pltpu.VMEM((2, 4, CAP, ROWS), F32),
            pltpu.VMEM((2, 4, CAP, ROWS), BF),
            pltpu.VMEM((2, 4, 1, ROWS), F32),
            dma((8,)),
            dma((2,)), dma((2,)), dma((2,)), dma((2,)), dma((2,)), dma((2,)), dma((2, 2)), dma((2, 2)), dma, dma,
            dma((LOCAL,)), dma((LOCAL,)), dma((LOCAL,)), dma((LOCAL,)),
            dma((7,)),
        ],
        compiler_params=pltpu.CompilerParams(
            collective_id=0, has_side_effects=True, vmem_limit_bytes=64 * 1024 * 1024
        ),
        name="block",
    )(
        caption_len, frames_in, modulation, caption_kv.T,
        w_spatial_qkv, w_spatial_proj, w_temporal_qkv, w_temporal_proj, w_cross_q, w_cross_out,
    )
    return out.reshape(frames_in.shape)


def solution(mesh):
    in_specs = (
        P(("dp", "seq"), None, None),
        P("dp", None),
        P("dp", "seq"),
        P("dp"),
        P(),
        P(),
        P(),
        P(),
        P("seq", None),
        P("seq", None),
    )
    out_specs = P(("dp", "seq"), None, None)
    return jax.shard_map(shards, mesh=mesh, in_specs=in_specs, out_specs=out_specs, check_vma=False)
```

```python
import math

import jax
import jax.numpy as jnp
from jax import lax
from jax.experimental import pallas as pl
from jax.experimental.pallas import tpu as pltpu
from jax.sharding import PartitionSpec as P

HEADS = 16
HEAD = 72
D = 1152
LANES = 128
SEQ = 32
LOCAL = 3
PATCH = 8
CAP = 120
ROWS = 256
HALVES = ((0, 640), (640, D))
BF = jnp.bfloat16
F32 = jnp.float32
MESH = pl.DeviceIdType.MESH
EXP_SCALE = HEAD ** (-0.5) * math.log2(math.e)


def window(head):
    low = HEAD * head
    return low // LANES * LANES, -(-(low + HEAD) // LANES) * LANES


def dot_nt(a, b):
    return lax.dot_general(a, b, (((1,), (1,)), ((), ())), preferred_element_type=F32)


def dot_nn(a, b):
    return jnp.dot(a, b, preferred_element_type=F32)


def head_mask(head):
    first, last = window(head)
    lane = lax.broadcasted_iota(jnp.int32, (1, last - first), 1) + first
    return jnp.where((lane >= HEAD * head) & (lane < HEAD * (head + 1)), 1.0, 0.0).astype(BF)


def placed(head):
    first, last = window(head)
    shape = (HEAD, last - first)
    feature = lax.broadcasted_iota(jnp.int32, shape, 0)
    lane = lax.broadcasted_iota(jnp.int32, shape, 1) + first
    return jnp.where(lane == feature + HEAD * head, 1.0, 0.0).astype(BF)


def frame_to_patch():
    row = lax.broadcasted_iota(jnp.int32, (ROWS, ROWS), 0)
    column = lax.broadcasted_iota(jnp.int32, (ROWS, ROWS), 1)
    return jnp.where(column == (row % SEQ) * PATCH + row // SEQ, 1.0, 0.0).astype(BF)


def patch_to_frame():
    row = lax.broadcasted_iota(jnp.int32, (ROWS, ROWS), 0)
    column = lax.broadcasted_iota(jnp.int32, (ROWS, ROWS), 1)
    return jnp.where(column == (row % PATCH) * SEQ + row // PATCH, 1.0, 0.0).astype(BF)


def spans(first, last, step=512):
    return [(c, min(c + step, last)) for c in range(first, last, step)]


def attend_heads(score, value_t, store, buffers, group, allowed=None):
    scores, weights, inverse = buffers
    groups = HEADS // group

    def multiply(g):
        for i in range(group):
            scores[g % 2, i] = score(g * group + i)

    def soften(g):
        for i in range(group):
            rows = scores[g % 2, i]
            if allowed is not None:
                rows = jnp.where(allowed, rows, -1e30)
            top = jnp.max(rows, axis=0, keepdims=True)
            raised = jnp.exp2((rows - top) * EXP_SCALE)
            inverse[g % 2, i] = 1.0 / jnp.sum(raised, axis=0, keepdims=True)
            weights[g % 2, i] = raised.astype(BF)

    def mix(g):
        for i in range(group):
            store(g * group + i, dot_nn(value_t(g * group + i), weights[g % 2, i]) * inverse[g % 2, i])

    multiply(0)
    for g in range(groups):
        if g + 1 < groups:
            multiply(g + 1)
        soften(g)
        mix(g)


def landed(ref, semaphore):
    pltpu.make_async_copy(ref, ref, semaphore).wait()


def kernel(
    caption_len, frames_ref, modulation, caption_ref, wsqkv_ref, wsp_ref, wtqkv_ref, wtp_ref, wcq_ref, wco_ref,
    out_ref,
    frames, wsqkv, wsp, wtqkv, wtp, wy, wg, cap, cap_keys,
    modulated, qk, vt, mix_t, mix, sent, received, x, tqk, tv, tvt, tmix_t, tmix,
    scores, weights, inverse, tscores, tweights, tinverse, cscores, cweights, cinverse,
    load_sem, y_send, y_recv, g_send, g_recv, z_send, z_recv, s_send, s_recv, c_send, c_recv,
    f_send, f_recv, r_send, r_recv, local_sem,
):
    me = lax.axis_index("seq")
    dp = lax.axis_index("dp")
    core = dp % 2
    my_x, my_z, my_y = me // 8, (me // 4) % 2, me % 4
    other_core = dp + 1 - 2 * core
    across = (dp + 2) % 4

    def peer_of(k):
        y = (my_y + k % 4) % 4
        x_ = (my_x + (k // 4) % 4) % 4
        z = (my_z + k // 16) % 2
        return x_ * 8 + z * 4 + y

    facing = my_x * 8 + (1 - my_z) * 4 + my_y

    barrier = pltpu.get_barrier_semaphore()

    @pl.loop(1, SEQ)
    def _(k):
        pl.semaphore_signal(barrier, inc=1, device_id={"seq": peer_of(k)}, device_id_type=MESH)

    pl.semaphore_signal(barrier, inc=1, device_id={"dp": other_core}, device_id_type=MESH)
    pl.semaphore_signal(barrier, inc=1, device_id={"dp": across, "seq": facing}, device_id_type=MESH)

    def load(i):
        source, target = [
            (frames_ref.at[0], frames.at[0]),
            (wsqkv_ref.at[:, :1024], wsqkv.at[:, :1024]),
            (wsqkv_ref.at[:, 1024 : 2 * D], wsqkv.at[:, 1024 : 2 * D]),
            (wsqkv_ref.at[:, 2 * D :], wsqkv.at[:, 2 * D :]),
            (wsp_ref, wsp),
            (frames_ref.at[pl.ds(1, 2)], frames.at[pl.ds(1, 2)]),
            (wtqkv_ref, wtqkv),
            (wtp_ref, wtp),
        ][i]
        return pltpu.make_async_copy(source, target, load_sem.at[i])

    for i in range(3):
        load(i).start()
    own_caption = pltpu.make_async_copy(caption_ref, cap.at[me], local_sem.at[0])
    own_caption.start()

    def by_core(step):
        for c in range(2):
            @pl.when(core == c)
            def _():
                step(c, slice(*HALVES[c]))

    def own_weight(m, columns):
        source = (wcq_ref, wco_ref)[m].at[:, columns]
        return pltpu.make_async_copy(source, wy.at[m, my_x * 4 + my_y, :, columns], local_sem.at[5 + m])

    def first_gather(c, columns):
        for m in range(2):
            own_weight(m, columns).start()

        for m, source in enumerate((wcq_ref, wco_ref)):
            @pl.loop(1, 4)
            def _(k):
                peer = (my_x + c * k) % 4 * 8 + my_z * 4 + (my_y + (1 - c) * k) % 4
                pltpu.make_async_remote_copy(
                    source.at[:, columns], wy.at[m, my_x * 4 + my_y, :, columns], y_send.at[m], y_recv.at[m],
                    device_id={"seq": peer}, device_id_type=MESH,
                ).start()

    def group_slot(c, i):
        return my_x * 4 + i if c == 0 else i * 4 + my_y

    def face_gather(c, columns):
        own_weight(1, columns).wait()
        landed(wy.at[1, pl.ds(0, 3), :, columns], y_recv.at[1])

        @pl.loop(0, 4)
        def _(i):
            pltpu.make_async_remote_copy(
                wy.at[1, group_slot(c, i), :, columns], wy.at[2, group_slot(c, i), :, columns],
                z_send.at[1], z_recv.at[1], device_id={"dp": across, "seq": facing}, device_id_type=MESH,
            ).start()

    def second_gather(m):
        def step(c, columns):
            if m == 0:
                own_weight(0, columns).wait()
                landed(wy.at[0, pl.ds(0, 3), :, columns], y_recv.at[0])
            else:
                landed(wy.at[2, pl.ds(0, 4), :, columns], z_recv.at[1])

            @pl.loop(0, 12 * (m + 1))
            def _(n):
                k, i = 1 + n // 4 % 3, n % 4
                block = wy.at[m + n // 12, group_slot(c, i), :, columns]
                peer = (my_x + (1 - c) * k) % 4 * 8 + my_z * 4 + (my_y + c * k) % 4
                pltpu.make_async_remote_copy(
                    block, block, g_send.at[m], g_recv.at[m], device_id={"seq": peer}, device_id_type=MESH
                ).start()

        by_core(step)

    def swap(m, block, half, columns):
        part = wg.at[m, block, :, columns]
        return pltpu.make_async_remote_copy(
            part, part, s_send.at[m, half], s_recv.at[m, half], device_id={"dp": other_core}, device_id_type=MESH
        )

    def third_gather(m):
        def step(c, columns):
            landed(wy.at[pl.ds(m, m + 1), pl.ds(0, 12), :, columns], g_recv.at[m])
            for plane in range(m, 2 * m + 1):
                for group in range(4):
                    block = group * 2 + (my_z if plane == m else 1 - my_z)
                    for y in range(4):
                        wg[m, block, 36 * y : 36 * (y + 1), columns] = wy[plane, group * 4 + y, :, columns]
            for group in range(4):
                if m == 0:
                    block = wg.at[0, group * 2 + my_z, :, columns]
                    pltpu.make_async_remote_copy(
                        block, block, z_send.at[0], z_recv.at[0],
                        device_id={"dp": across, "seq": facing}, device_id_type=MESH,
                    ).start()
                else:
                    swap(1, group * 2 + 1 - my_z, 1, columns).start()
                swap(m, group * 2 + my_z, 0, columns).start()

        by_core(step)

    def last_gather(c, columns):
        landed(wg.at[0, pl.ds(0, 4), :, columns], z_recv.at[0])
        for group in range(4):
            swap(0, group * 2 + 1 - my_z, 1, columns).start()

    def whole_weight(m):
        def step(c, columns):
            for half in range(2):
                landed(wg.at[m, pl.ds(0, 4), :, slice(*HALVES[1 - c])], s_recv.at[m, half])

        by_core(step)

    def sent_weights(c, columns):
        landed(wg.at[0, pl.ds(0, 4), :, columns], z_send.at[0])
        landed(wy.at[2, pl.ds(0, 4), :, columns], z_send.at[1])
        for m in range(2):
            landed(wy.at[m, pl.ds(0, 3), :, columns], y_send.at[m])
            landed(wy.at[pl.ds(m, m + 1), pl.ds(0, 12), :, columns], g_send.at[m])
            for half in range(2):
                landed(wg.at[m, pl.ds(0, 4), :, columns], s_send.at[m, half])

    pl.semaphore_wait(barrier, SEQ + 1)

    by_core(first_gather)

    def spatial(f, _):
        @pl.when(f == 0)
        def _():
            load(0).wait()

        @pl.when(f == 1)
        def _():
            load(5).wait()

        @pl.loop(0, ROWS // 32, unroll=4)
        def _(r):
            rows = pl.ds(pl.multiple_of(r * 32, 32), 32)
            wide = frames[f, rows, :].astype(F32)
            centered = wide - jnp.mean(wide, axis=-1, keepdims=True)
            variance = jnp.mean(centered * centered, axis=-1, keepdims=True)
            normed = centered * lax.rsqrt(variance + 1e-06)
            modulated[rows, :] = (normed * (1.0 + modulation[1:2, :]) + modulation[0:1, :]).astype(BF)

        @pl.when(f == 0)
        def _():
            load(1).wait()
            load(3).start()
            load(4).start()

        for first, last in spans(0, 1024):
            qk[:, first:last] = dot_nn(modulated[...], wsqkv[:, first:last]).astype(BF)

        @pl.when(f == 0)
        def _():
            load(2).wait()
            load(5).start()
            second_gather(0)
            by_core(face_gather)

        for first, last in spans(1024, 2 * D):
            qk[:, first:last] = dot_nn(modulated[...], wsqkv[:, first:last]).astype(BF)

        @pl.when(f == 0)
        def _():
            load(3).wait()
            load(6).start()

        for first, last in spans(0, D):
            vt[first:last, :] = dot_nn(modulated[...], wsqkv[:, 2 * D + first : 2 * D + last]).T

        def score(head):
            first, last = window(head)
            return dot_nt(qk[:, D + first : D + last] * head_mask(head), qk[:, first:last])

        def store(head, rows):
            mix_t[HEAD * head : HEAD * (head + 1), :] = rows

        attend_heads(
            score, lambda head: vt[HEAD * head : HEAD * (head + 1), :].astype(BF), store, (scores, weights, inverse), 4
        )
        for first, last in spans(0, D):
            mix[:, first:last] = mix_t[first:last, :].T.astype(BF)

        @pl.when(f == 1)
        def _():
            third_gather(0)

        @pl.when(f == 0)
        def _():
            load(4).wait()
            load(7).start()

        for first, last in spans(0, D):
            branch = dot_nn(mix[...], wsp[:, first:last])
            after = frames[f, :, first:last].astype(F32) + modulation[2:3, first:last] * branch
            sent[f, :, :, first:last] = after.reshape(SEQ, PATCH, last - first).astype(BF)

        @pl.loop(1, SEQ)
        def _(k):
            peer = peer_of(k)
            pltpu.make_async_remote_copy(
                sent.at[f, peer], received.at[f, me], f_send.at[f], f_recv.at[f],
                device_id={"seq": peer}, device_id_type=MESH,
            ).start()

        received[f, me] = sent[f, me]
        return 0

    lax.fori_loop(0, LOCAL, spatial, 0)
    second_gather(1)

    @pl.loop(1, SEQ)
    def _(k):
        pltpu.make_async_remote_copy(
            caption_ref, cap.at[me], c_send, c_recv, device_id={"seq": peer_of(k)}, device_id_type=MESH
        ).start()

    def temporal_qkv(f, _):
        landed(received.at[f, pl.ds(0, SEQ - 1)], f_recv.at[f])

        @pl.when(f == 0)
        def _():
            load(6).wait()

        order = frame_to_patch()
        for first, last in spans(0, D):
            block = received[f, :, :, first:last].astype(F32).reshape(ROWS, last - first).astype(BF)
            x[f, :, first:last] = dot_nn(order, block).astype(BF)
        frame_rows = pl.ds(pl.multiple_of(f * SEQ, SEQ), SEQ)
        for first, last in spans(0, 2 * D):
            product = dot_nn(x[f], wtqkv[:, first:last]).astype(BF)
            tqk[:, frame_rows, first:last] = product.reshape(PATCH, SEQ, last - first)
        for first, last in spans(0, D):
            product = dot_nn(x[f], wtqkv[:, 2 * D + first : 2 * D + last]).astype(BF)
            tv[:, frame_rows, first:last] = product.reshape(PATCH, SEQ, last - first)

        return 0

    lax.fori_loop(0, LOCAL, temporal_qkv, 0)
    by_core(last_gather)

    frames_all = LOCAL * SEQ

    def temporal(p, _):
        for first, last in spans(0, D, 384):
            tvt[first:last, :] = tv[p, :, first:last].astype(F32).T

        def score(head):
            first, last = window(head)
            return dot_nt(tqk[p, :, D + first : D + last] * head_mask(head), tqk[p, :, first:last])

        def store(head, rows):
            tmix_t[HEAD * head : HEAD * (head + 1), :frames_all] = rows

        attend_heads(
            score, lambda head: tvt[HEAD * head : HEAD * (head + 1), :frames_all].astype(BF), store,
            (tscores, tweights, tinverse), 8,
        )
        for first, last in spans(0, D, 384):
            block = tmix_t[first:last, :].T.astype(BF)
            for f in range(LOCAL):
                tmix[f, pl.ds(pl.multiple_of(p * SEQ, SEQ), SEQ), first:last] = block[f * SEQ : (f + 1) * SEQ]

        @pl.when(p == 6)
        def _():
            third_gather(1)

        return 0

    tv[:, frames_all:, :] = jnp.zeros((PATCH, LANES - frames_all, D), BF)
    tmix_t[...] = jnp.zeros((D, LANES), F32)
    lax.fori_loop(0, PATCH, temporal, 0)

    load(7).wait()
    for f in range(LOCAL):
        landed(sent.at[f, pl.ds(0, SEQ - 1)], f_send.at[f])

    def finish(f, _):
        after = modulated
        for first, last in spans(0, D):
            branch = dot_nn(tmix[f], wtp[:, first:last])
            after[:, first:last] = (
                x[f, :, first:last].astype(F32) + modulation[2:3, first:last] * branch
            ).astype(BF)

        @pl.when(f == 0)
        def _():
            whole_weight(0)

        for first, last in spans(0, D):
            qk[:, first:last] = dot_nn(after[...], wg[0, :, :, first:last].reshape(D, last - first)).astype(BF)

        @pl.when(f == 0)
        def _():
            own_caption.wait()
            landed(cap.at[pl.ds(0, SEQ - 1)], c_recv)
            for head in range(HEADS):
                first, last = window(head)
                cap_keys[head, :, : last - first] = lax.dot_general(
                    cap[head], placed(head), (((0,), (0,)), ((), ())), preferred_element_type=F32
                ).astype(BF)

        def score(head):
            first, last = window(head)
            return dot_nt(cap_keys[head, :, : last - first], qk[:, first:last])

        def store(head, rows):
            mix_t[HEAD * head : HEAD * (head + 1), :] = rows

        allowed = lax.broadcasted_iota(jnp.int32, (CAP, ROWS), 0) < caption_len[0]
        attend_heads(score, lambda head: cap[HEADS + head], store, (cscores, cweights, cinverse), 4, allowed)
        for first, last in spans(0, D):
            mix[:, first:last] = mix_t[first:last, :].T.astype(BF)

        @pl.when(f == 0)
        def _():
            whole_weight(1)

        order = patch_to_frame()
        for first, last in spans(0, D):
            branch = dot_nn(mix[...], wg[1, :, :, first:last].reshape(D, last - first))
            rows = (after[:, first:last].astype(F32) + branch).astype(BF)
            sent[f, :, :, first:last] = dot_nn(order, rows).reshape(SEQ, PATCH, last - first).astype(BF)

        @pl.loop(1, SEQ)
        def _(k):
            peer = peer_of(k)
            pltpu.make_async_remote_copy(
                sent.at[f, peer], out_ref.at[f, me], r_send.at[f], r_recv.at[f],
                device_id={"seq": peer}, device_id_type=MESH,
            ).start()

        pltpu.make_async_copy(sent.at[f, me], out_ref.at[f, me], local_sem.at[2 + f]).start()
        return 0

    lax.fori_loop(0, LOCAL, finish, 0)

    for f in range(LOCAL):
        pltpu.make_async_copy(sent.at[f, me], out_ref.at[f, me], local_sem.at[2 + f]).wait()
        landed(sent.at[f, pl.ds(0, SEQ - 1)], r_send.at[f])
        landed(out_ref.at[f, pl.ds(0, SEQ - 1)], r_recv.at[f])
    by_core(sent_weights)
    landed(cap.at[pl.ds(0, SEQ - 1)], c_send)


def shards(
    frames_in, modulation, caption_kv, caption_len,
    w_spatial_qkv, w_spatial_proj, w_temporal_qkv, w_temporal_proj, w_cross_q, w_cross_out,
):
    vmem = pl.BlockSpec(memory_space=pltpu.VMEM)
    whole = pl.BlockSpec(memory_space=pl.ANY)
    dma = pltpu.SemaphoreType.DMA
    out = pl.pallas_call(
        kernel,
        out_shape=pltpu.VMEM((LOCAL, SEQ, PATCH, D), BF),
        in_specs=[pl.BlockSpec(memory_space=pltpu.SMEM), whole, vmem] + [whole] * 7,
        out_specs=whole,
        scratch_shapes=[
            pltpu.VMEM((LOCAL, ROWS, D), BF),
            pltpu.VMEM((D, 3 * D), BF),
            pltpu.VMEM((D, D), BF),
            pltpu.VMEM((D, 3 * D), BF),
            pltpu.VMEM((D, D), BF),
            pltpu.VMEM((3, 16, 36, D), BF),
            pltpu.VMEM((2, 8, 144, D), BF),
            pltpu.VMEM((SEQ, HEAD, CAP), BF),
            pltpu.VMEM((HEADS, CAP, 2 * LANES), BF),
            pltpu.VMEM((ROWS, D), BF),
            pltpu.VMEM((ROWS, 2 * D), BF),
            pltpu.VMEM((D, ROWS), F32),
            pltpu.VMEM((D, ROWS), F32),
            pltpu.VMEM((ROWS, D), BF),
            pltpu.VMEM((LOCAL, SEQ, PATCH, D), BF),
            pltpu.VMEM((LOCAL, SEQ, PATCH, D), BF),
            pltpu.VMEM((LOCAL, ROWS, D), BF),
            pltpu.VMEM((PATCH, LOCAL * SEQ, 2 * D), BF),
            pltpu.VMEM((PATCH, LANES, D), BF),
            pltpu.VMEM((D, LANES), F32),
            pltpu.VMEM((D, LANES), F32),
            pltpu.VMEM((LOCAL, ROWS, D), BF),
            pltpu.VMEM((2, 4, ROWS, ROWS), F32),
            pltpu.VMEM((2, 4, ROWS, ROWS), BF),
            pltpu.VMEM((2, 4, 1, ROWS), F32),
            pltpu.VMEM((2, 8, LOCAL * SEQ, LOCAL * SEQ), F32),
            pltpu.VMEM((2, 8, LOCAL * SEQ, LOCAL * SEQ), BF),
            pltpu.VMEM((2, 8, 1, LOCAL * SEQ), F32),
            pltpu.VMEM((2, 4, CAP, ROWS), F32),
            pltpu.VMEM((2, 4, CAP, ROWS), BF),
            pltpu.VMEM((2, 4, 1, ROWS), F32),
            dma((8,)),
            dma((2,)), dma((2,)), dma((2,)), dma((2,)), dma((2,)), dma((2,)), dma((2, 2)), dma((2, 2)), dma, dma,
            dma((LOCAL,)), dma((LOCAL,)), dma((LOCAL,)), dma((LOCAL,)),
            dma((7,)),
        ],
        compiler_params=pltpu.CompilerParams(
            collective_id=0, has_side_effects=True, vmem_limit_bytes=60 * 1024 * 1024
        ),
        name="block",
    )(
        caption_len, frames_in, modulation, caption_kv.T,
        w_spatial_qkv, w_spatial_proj, w_temporal_qkv, w_temporal_proj, w_cross_q, w_cross_out,
    )
    return out.reshape(frames_in.shape)


def solution(mesh):
    in_specs = (
        P(("dp", "seq"), None, None),
        P("dp", None),
        P("dp", "seq"),
        P("dp"),
        P(),
        P(),
        P(),
        P(),
        P("seq", None),
        P("seq", None),
    )
    out_specs = P(("dp", "seq"), None, None)
    return jax.shard_map(shards, mesh=mesh, in_specs=in_specs, out_specs=out_specs, check_vma=False)
```

```python
import math

import jax
import jax.numpy as jnp
from jax import lax
from jax.experimental import pallas as pl
from jax.experimental.pallas import tpu as pltpu
from jax.sharding import PartitionSpec as P

HEADS = 16
HEAD = 72
D = 1152
LANES = 128
SEQ = 32
LOCAL = 3
PATCH = 8
CAP = 120
ROWS = 256
HALF = 128
HALVES = ((0, 640), (640, D))
BF = jnp.bfloat16
F32 = jnp.float32
MESH = pl.DeviceIdType.MESH
EXP_SCALE = HEAD ** (-0.5) * math.log2(math.e)


def window(head):
    low = HEAD * head
    return low // LANES * LANES, -(-(low + HEAD) // LANES) * LANES


def dot_nt(a, b):
    return lax.dot_general(a, b, (((1,), (1,)), ((), ())), preferred_element_type=F32)


def dot_nn(a, b):
    return jnp.dot(a, b, preferred_element_type=F32)


def head_mask(head):
    first, last = window(head)
    lane = lax.broadcasted_iota(jnp.int32, (1, last - first), 1) + first
    return jnp.where((lane >= HEAD * head) & (lane < HEAD * (head + 1)), 1.0, 0.0).astype(BF)


def placed(head):
    first, last = window(head)
    shape = (HEAD, last - first)
    feature = lax.broadcasted_iota(jnp.int32, shape, 0)
    lane = lax.broadcasted_iota(jnp.int32, shape, 1) + first
    return jnp.where(lane == feature + HEAD * head, 1.0, 0.0).astype(BF)


def frame_to_patch():
    row = lax.broadcasted_iota(jnp.int32, (HALF, HALF), 0)
    column = lax.broadcasted_iota(jnp.int32, (HALF, HALF), 1)
    return jnp.where(column == (row % 16) * PATCH + row // 16, 1.0, 0.0).astype(BF)


def patch_to_frame():
    row = lax.broadcasted_iota(jnp.int32, (HALF, HALF), 0)
    column = lax.broadcasted_iota(jnp.int32, (HALF, HALF), 1)
    return jnp.where(column == (row % PATCH) * 16 + row // PATCH, 1.0, 0.0).astype(BF)


def spans(first, last, step=512):
    return [(c, min(c + step, last)) for c in range(first, last, step)]


def attend_heads(score, value_t, store, buffers, group, allowed=None):
    scores, weights, inverse = buffers
    groups = HEADS // group

    def multiply(g):
        for i in range(group):
            scores[g % 2, i] = score(g * group + i)

    def soften(g):
        for i in range(group):
            rows = scores[g % 2, i]
            if allowed is not None:
                rows = jnp.where(allowed, rows, -1e30)
            top = jnp.max(rows, axis=0, keepdims=True)
            raised = jnp.exp2((rows - top) * EXP_SCALE)
            inverse[g % 2, i] = 1.0 / jnp.sum(raised, axis=0, keepdims=True)
            weights[g % 2, i] = raised.astype(BF)

    def mix(g):
        for i in range(group):
            store(g * group + i, dot_nn(value_t(g * group + i), weights[g % 2, i]) * inverse[g % 2, i])

    multiply(0)
    for g in range(groups):
        if g + 1 < groups:
            multiply(g + 1)
        soften(g)
        mix(g)


def landed(ref, semaphore):
    pltpu.make_async_copy(ref, ref, semaphore).wait()


def kernel(
    caption_len, frames_ref, modulation, caption_ref, wsqkv_ref, wsp_ref, wtqkv_ref, wtp_ref, wcq_ref, wco_ref,
    out_ref,
    frames, wsqkv, wsp, wtqkv, wtp, wy, wg, cap, cap_keys,
    modulated, qk, vt, mix_t, mix, sent, received, x, tqk, tv, tvt, tmix_t, tmix,
    scores, weights, inverse, tscores, tweights, tinverse, cscores, cweights, cinverse,
    load_sem, y_send, y_recv, g_send, g_recv, z_send, z_recv, s_send, s_recv, c_send, c_recv,
    f_send, f_recv, r_send, r_recv, local_sem,
):
    me = lax.axis_index("seq")
    dp = lax.axis_index("dp")
    core = dp % 2
    my_x, my_z, my_y = me // 8, (me // 4) % 2, me % 4
    other_core = dp + 1 - 2 * core
    across = (dp + 2) % 4

    def peer_of(k):
        y = (my_y + k % 4) % 4
        x_ = (my_x + (k // 4) % 4) % 4
        z = (my_z + k // 16) % 2
        return x_ * 8 + z * 4 + y

    def place_of(x_, z, y):
        return (x_ + z + y) % 2 * 16 + x_ * 4 + z * 2 + y // 2

    my_place = place_of(my_x, my_z, my_y)
    my_parity = my_place // 16

    def parity_peer(turn, n):
        k_x, k_z = n // 4, n // 2 % 2
        k_y = n % 2 * 2 + (k_x + k_z + 1 + turn) % 2
        x_, z, y = (my_x + k_x) % 4, (my_z + k_z) % 2, (my_y + k_y) % 4
        return x_ * 8 + z * 4 + y, place_of(x_, z, y)

    facing = my_x * 8 + (1 - my_z) * 4 + my_y

    barrier = pltpu.get_barrier_semaphore()

    @pl.loop(1, SEQ)
    def _(k):
        pl.semaphore_signal(barrier, inc=1, device_id={"seq": peer_of(k)}, device_id_type=MESH)

    pl.semaphore_signal(barrier, inc=1, device_id={"dp": other_core}, device_id_type=MESH)
    pl.semaphore_signal(barrier, inc=1, device_id={"dp": across, "seq": facing}, device_id_type=MESH)

    def load(i):
        source, target = [
            (frames_ref.at[0], frames.at[0]),
            (wsqkv_ref.at[:, :1024], wsqkv.at[:, :1024]),
            (wsqkv_ref.at[:, 1024 : 2 * D], wsqkv.at[:, 1024 : 2 * D]),
            (wsqkv_ref.at[:, 2 * D :], wsqkv.at[:, 2 * D :]),
            (wsp_ref, wsp),
            (frames_ref.at[pl.ds(1, 2)], frames.at[pl.ds(1, 2)]),
            (wtqkv_ref, wtqkv),
            (wtp_ref, wtp),
        ][i]
        return pltpu.make_async_copy(source, target, load_sem.at[i])

    for i in range(3):
        load(i).start()
    own_caption = pltpu.make_async_copy(caption_ref, cap.at[me], local_sem.at[0])
    own_caption.start()

    def by_core(step):
        for c in range(2):
            @pl.when(core == c)
            def _():
                step(c, slice(*HALVES[c]))

    def own_weight(m, columns):
        source = (wcq_ref, wco_ref)[m].at[:, columns]
        return pltpu.make_async_copy(source, wy.at[m, my_x * 4 + my_y, :, columns], local_sem.at[5 + m])

    def first_gather(c, columns):
        for m in range(2):
            own_weight(m, columns).start()

        for m, source in enumerate((wcq_ref, wco_ref)):
            @pl.loop(1, 4)
            def _(k):
                peer = (my_x + c * k) % 4 * 8 + my_z * 4 + (my_y + (1 - c) * k) % 4
                pltpu.make_async_remote_copy(
                    source.at[:, columns], wy.at[m, my_x * 4 + my_y, :, columns], y_send.at[m], y_recv.at[m],
                    device_id={"seq": peer}, device_id_type=MESH,
                ).start()

    def group_slot(c, i):
        return my_x * 4 + i if c == 0 else i * 4 + my_y

    def face_gather(c, columns):
        own_weight(1, columns).wait()
        landed(wy.at[1, pl.ds(0, 3), :, columns], y_recv.at[1])

        @pl.loop(0, 4)
        def _(i):
            pltpu.make_async_remote_copy(
                wy.at[1, group_slot(c, i), :, columns], wy.at[2, group_slot(c, i), :, columns],
                z_send.at[1], z_recv.at[1], device_id={"dp": across, "seq": facing}, device_id_type=MESH,
            ).start()

    def second_gather(m):
        def step(c, columns):
            if m == 0:
                own_weight(0, columns).wait()
                landed(wy.at[0, pl.ds(0, 3), :, columns], y_recv.at[0])
            else:
                landed(wy.at[2, pl.ds(0, 4), :, columns], z_recv.at[1])

            @pl.loop(0, 12 * (m + 1))
            def _(n):
                k, i = 1 + n // 4 % 3, n % 4
                block = wy.at[m + n // 12, group_slot(c, i), :, columns]
                peer = (my_x + (1 - c) * k) % 4 * 8 + my_z * 4 + (my_y + c * k) % 4
                pltpu.make_async_remote_copy(
                    block, block, g_send.at[m], g_recv.at[m], device_id={"seq": peer}, device_id_type=MESH
                ).start()

        by_core(step)

    def swap(m, block, half, columns):
        part = wg.at[m, block, :, columns]
        return pltpu.make_async_remote_copy(
            part, part, s_send.at[m, half], s_recv.at[m, half], device_id={"dp": other_core}, device_id_type=MESH
        )

    def third_gather(m):
        def step(c, columns):
            landed(wy.at[pl.ds(m, m + 1), pl.ds(0, 12), :, columns], g_recv.at[m])
            for plane in range(m, 2 * m + 1):
                for group in range(4):
                    block = group * 2 + (my_z if plane == m else 1 - my_z)
                    for y in range(4):
                        wg[m, block, 36 * y : 36 * (y + 1), columns] = wy[plane, group * 4 + y, :, columns]
            for group in range(4):
                if m == 0:
                    block = wg.at[0, group * 2 + my_z, :, columns]
                    pltpu.make_async_remote_copy(
                        block, block, z_send.at[0], z_recv.at[0],
                        device_id={"dp": across, "seq": facing}, device_id_type=MESH,
                    ).start()
                else:
                    swap(1, group * 2 + 1 - my_z, 1, columns).start()
                swap(m, group * 2 + my_z, 0, columns).start()

        by_core(step)

    def last_gather(c, columns):
        landed(wg.at[0, pl.ds(0, 4), :, columns], z_recv.at[0])
        for group in range(4):
            swap(0, group * 2 + 1 - my_z, 1, columns).start()

    def whole_weight(m):
        def step(c, columns):
            for half in range(2):
                landed(wg.at[m, pl.ds(0, 4), :, slice(*HALVES[1 - c])], s_recv.at[m, half])

        by_core(step)

    def sent_weights(c, columns):
        landed(wg.at[0, pl.ds(0, 4), :, columns], z_send.at[0])
        landed(wy.at[2, pl.ds(0, 4), :, columns], z_send.at[1])
        for m in range(2):
            landed(wy.at[m, pl.ds(0, 3), :, columns], y_send.at[m])
            landed(wy.at[pl.ds(m, m + 1), pl.ds(0, 12), :, columns], g_send.at[m])
            for half in range(2):
                landed(wg.at[m, pl.ds(0, 4), :, columns], s_send.at[m, half])

    pl.semaphore_wait(barrier, SEQ + 1)

    by_core(first_gather)

    def spatial(f, _):
        @pl.when(f == 0)
        def _():
            load(0).wait()

        @pl.when(f == 1)
        def _():
            load(5).wait()

        @pl.loop(0, ROWS // 32, unroll=4)
        def _(r):
            rows = pl.ds(pl.multiple_of(r * 32, 32), 32)
            wide = frames[f, rows, :].astype(F32)
            centered = wide - jnp.mean(wide, axis=-1, keepdims=True)
            variance = jnp.mean(centered * centered, axis=-1, keepdims=True)
            normed = centered * lax.rsqrt(variance + 1e-06)
            modulated[rows, :] = (normed * (1.0 + modulation[1:2, :]) + modulation[0:1, :]).astype(BF)

        @pl.when(f == 0)
        def _():
            load(1).wait()
            load(3).start()
            load(4).start()

        for first, last in spans(0, 1024):
            qk[:, first:last] = dot_nn(modulated[...], wsqkv[:, first:last]).astype(BF)

        @pl.when(f == 0)
        def _():
            load(2).wait()
            load(5).start()
            second_gather(0)
            by_core(face_gather)

        for first, last in spans(1024, 2 * D):
            qk[:, first:last] = dot_nn(modulated[...], wsqkv[:, first:last]).astype(BF)

        @pl.when(f == 0)
        def _():
            load(3).wait()
            load(6).start()

        for first, last in spans(0, D):
            vt[first:last, :] = dot_nn(modulated[...], wsqkv[:, 2 * D + first : 2 * D + last]).T

        def score(head):
            first, last = window(head)
            return dot_nt(qk[:, D + first : D + last] * head_mask(head), qk[:, first:last])

        def store(head, rows):
            mix_t[HEAD * head : HEAD * (head + 1), :] = rows

        attend_heads(
            score, lambda head: vt[HEAD * head : HEAD * (head + 1), :].astype(BF), store, (scores, weights, inverse), 4
        )
        for first, last in spans(0, D):
            mix[:, first:last] = mix_t[first:last, :].T.astype(BF)

        @pl.when(f == 1)
        def _():
            third_gather(0)

        @pl.when(f == 0)
        def _():
            load(4).wait()
            load(7).start()

        for first, last in spans(0, D):
            branch = dot_nn(mix[...], wsp[:, first:last])
            after = frames[f, :, first:last].astype(F32) + modulation[2:3, first:last] * branch
            sent[f, :, :, first:last] = after.reshape(SEQ, PATCH, last - first).astype(BF)

        for turn in range(2):
            @pl.loop(turn, 16)
            def _(n):
                peer, _ = parity_peer(turn, n)
                pltpu.make_async_remote_copy(
                    sent.at[f, peer], received.at[f, my_place], f_send.at[f], f_recv.at[f, turn],
                    device_id={"seq": peer}, device_id_type=MESH,
                ).start()

        received[f, my_place] = sent[f, me]
        return 0

    lax.fori_loop(0, LOCAL, spatial, 0)
    second_gather(1)

    @pl.loop(1, SEQ)
    def _(k):
        pltpu.make_async_remote_copy(
            caption_ref, cap.at[me], c_send, c_recv, device_id={"seq": peer_of(k)}, device_id_type=MESH
        ).start()

    order = frame_to_patch()

    @pl.loop(0, LOCAL)
    def _(f):
        for turn in range(2):
            landed(received.at[f, pl.ds(0, 16 - turn)], f_recv.at[f, turn])

            if turn == 0:
                @pl.when(f == 0)
                def _():
                    load(6).wait()

            first_place = pl.multiple_of((my_parity + 1 + turn) % 2 * 16, 16)
            places = pl.ds(first_place, 16)
            for first, last in spans(0, D):
                block = received[f, places, :, first:last].astype(F32).reshape(HALF, last - first).astype(BF)
                block = dot_nn(order, block).astype(BF)
                modulated[:HALF, first:last] = block
                x[f, :, places, first:last] = block.reshape(PATCH, 16, last - first)
            frame_rows = pl.ds(pl.multiple_of(f * SEQ + first_place, 16), 16)
            for first, last in spans(0, 2 * D):
                product = dot_nn(modulated[:HALF, :], wtqkv[:, first:last]).astype(BF)
                tqk[:, frame_rows, first:last] = product.reshape(PATCH, 16, last - first)
            for first, last in spans(0, D):
                product = dot_nn(modulated[:HALF, :], wtqkv[:, 2 * D + first : 2 * D + last]).astype(BF)
                tv[:, frame_rows, first:last] = product.reshape(PATCH, 16, last - first)

    by_core(last_gather)

    frames_all = LOCAL * SEQ

    def temporal(p, _):
        for first, last in spans(0, D, 384):
            tvt[first:last, :] = tv[p, :, first:last].astype(F32).T

        def score(head):
            first, last = window(head)
            return dot_nt(tqk[p, :, D + first : D + last] * head_mask(head), tqk[p, :, first:last])

        def store(head, rows):
            tmix_t[HEAD * head : HEAD * (head + 1), :frames_all] = rows

        attend_heads(
            score, lambda head: tvt[HEAD * head : HEAD * (head + 1), :frames_all].astype(BF), store,
            (tscores, tweights, tinverse), 8,
        )
        for first, last in spans(0, D, 384):
            block = tmix_t[first:last, :].T.astype(BF)
            for f in range(LOCAL):
                tmix[f, p, :, first:last] = block[f * SEQ : (f + 1) * SEQ]
        return 0

    tv[:, frames_all:, :] = jnp.zeros((PATCH, LANES - frames_all, D), BF)
    tmix_t[...] = jnp.zeros((D, LANES), F32)
    lax.fori_loop(0, PATCH, temporal, 0)
    third_gather(1)

    load(7).wait()
    for f in range(LOCAL):
        landed(sent.at[f, pl.ds(0, SEQ - 1)], f_send.at[f])

    def finish(step, _):
        f, turn = step // 2, step % 2
        places = pl.ds(pl.multiple_of((my_parity + 1 + turn) % 2 * 16, 16), 16)
        after = modulated
        for first, last in spans(0, D):
            branch = dot_nn(tmix[f, :, places, :].reshape(HALF, D), wtp[:, first:last])
            after[:HALF, first:last] = (
                x[f, :, places, first:last].reshape(HALF, last - first).astype(F32) + modulation[2:3, first:last] * branch
            ).astype(BF)

        @pl.when(step == 0)
        def _():
            whole_weight(0)

        for first, last in spans(0, D):
            qk[:HALF, first:last] = dot_nn(after[:HALF, :], wg[0, :, :, first:last].reshape(D, last - first)).astype(BF)

        @pl.when(step == 0)
        def _():
            own_caption.wait()
            landed(cap.at[pl.ds(0, SEQ - 1)], c_recv)
            for head in range(HEADS):
                first, last = window(head)
                cap_keys[head, :, : last - first] = lax.dot_general(
                    cap[head], placed(head), (((0,), (0,)), ((), ())), preferred_element_type=F32
                ).astype(BF)

        def score(head):
            first, last = window(head)
            return dot_nt(cap_keys[head, :, : last - first], qk[:HALF, first:last])

        def store(head, rows):
            mix_t[HEAD * head : HEAD * (head + 1), :HALF] = rows

        allowed = lax.broadcasted_iota(jnp.int32, (CAP, HALF), 0) < caption_len[0]
        attend_heads(score, lambda head: cap[HEADS + head], store, (cscores, cweights, cinverse), 4, allowed)
        for first, last in spans(0, D):
            mix[:HALF, first:last] = mix_t[first:last, :HALF].T.astype(BF)

        @pl.when(step == 0)
        def _():
            whole_weight(1)

        order = patch_to_frame()
        for first, last in spans(0, D):
            branch = dot_nn(mix[:HALF, :], wg[1, :, :, first:last].reshape(D, last - first))
            rows = (after[:HALF, first:last].astype(F32) + branch).astype(BF)
            sent[f, places, :, first:last] = dot_nn(order, rows).reshape(16, PATCH, last - first).astype(BF)

        @pl.loop(turn, 16)
        def _(n):
            peer, place = parity_peer(turn, n)
            pltpu.make_async_remote_copy(
                sent.at[f, place], out_ref.at[f, me], r_send.at[f], r_recv.at[f],
                device_id={"seq": peer}, device_id_type=MESH,
            ).start()

        @pl.when(turn == 1)
        def _():
            pltpu.make_async_copy(sent.at[f, my_place], out_ref.at[f, me], local_sem.at[2 + f]).start()

        return 0

    lax.fori_loop(0, 2 * LOCAL, finish, 0)

    for f in range(LOCAL):
        pltpu.make_async_copy(sent.at[f, my_place], out_ref.at[f, me], local_sem.at[2 + f]).wait()
        landed(sent.at[f, pl.ds(0, SEQ - 1)], r_send.at[f])
        landed(out_ref.at[f, pl.ds(0, SEQ - 1)], r_recv.at[f])
    by_core(sent_weights)
    landed(cap.at[pl.ds(0, SEQ - 1)], c_send)


def shards(
    frames_in, modulation, caption_kv, caption_len,
    w_spatial_qkv, w_spatial_proj, w_temporal_qkv, w_temporal_proj, w_cross_q, w_cross_out,
):
    vmem = pl.BlockSpec(memory_space=pltpu.VMEM)
    whole = pl.BlockSpec(memory_space=pl.ANY)
    dma = pltpu.SemaphoreType.DMA
    out = pl.pallas_call(
        kernel,
        out_shape=pltpu.VMEM((LOCAL, SEQ, PATCH, D), BF),
        in_specs=[pl.BlockSpec(memory_space=pltpu.SMEM), whole, vmem] + [whole] * 7,
        out_specs=whole,
        scratch_shapes=[
            pltpu.VMEM((LOCAL, ROWS, D), BF),
            pltpu.VMEM((D, 3 * D), BF),
            pltpu.VMEM((D, D), BF),
            pltpu.VMEM((D, 3 * D), BF),
            pltpu.VMEM((D, D), BF),
            pltpu.VMEM((3, 16, 36, D), BF),
            pltpu.VMEM((2, 8, 144, D), BF),
            pltpu.VMEM((SEQ, HEAD, CAP), BF),
            pltpu.VMEM((HEADS, CAP, 2 * LANES), BF),
            pltpu.VMEM((ROWS, D), BF),
            pltpu.VMEM((ROWS, 2 * D), BF),
            pltpu.VMEM((D, ROWS), F32),
            pltpu.VMEM((D, ROWS), F32),
            pltpu.VMEM((ROWS, D), BF),
            pltpu.VMEM((LOCAL, SEQ, PATCH, D), BF),
            pltpu.VMEM((LOCAL, SEQ, PATCH, D), BF),
            pltpu.VMEM((LOCAL, PATCH, SEQ, D), BF),
            pltpu.VMEM((PATCH, LOCAL * SEQ, 2 * D), BF),
            pltpu.VMEM((PATCH, LANES, D), BF),
            pltpu.VMEM((D, LANES), F32),
            pltpu.VMEM((D, LANES), F32),
            pltpu.VMEM((LOCAL, PATCH, SEQ, D), BF),
            pltpu.VMEM((2, 4, ROWS, ROWS), F32),
            pltpu.VMEM((2, 4, ROWS, ROWS), BF),
            pltpu.VMEM((2, 4, 1, ROWS), F32),
            pltpu.VMEM((2, 8, LOCAL * SEQ, LOCAL * SEQ), F32),
            pltpu.VMEM((2, 8, LOCAL * SEQ, LOCAL * SEQ), BF),
            pltpu.VMEM((2, 8, 1, LOCAL * SEQ), F32),
            pltpu.VMEM((2, 4, CAP, HALF), F32),
            pltpu.VMEM((2, 4, CAP, HALF), BF),
            pltpu.VMEM((2, 4, 1, HALF), F32),
            dma((8,)),
            dma((2,)), dma((2,)), dma((2,)), dma((2,)), dma((2,)), dma((2,)), dma((2, 2)), dma((2, 2)), dma, dma,
            dma((LOCAL,)), dma((LOCAL, 2)), dma((LOCAL,)), dma((LOCAL,)),
            dma((7,)),
        ],
        compiler_params=pltpu.CompilerParams(
            collective_id=0, has_side_effects=True, vmem_limit_bytes=60 * 1024 * 1024
        ),
        name="block",
    )(
        caption_len, frames_in, modulation, caption_kv.T,
        w_spatial_qkv, w_spatial_proj, w_temporal_qkv, w_temporal_proj, w_cross_q, w_cross_out,
    )
    return out.reshape(frames_in.shape)


def solution(mesh):
    in_specs = (
        P(("dp", "seq"), None, None),
        P("dp", None),
        P("dp", "seq"),
        P("dp"),
        P(),
        P(),
        P(),
        P(),
        P("seq", None),
        P("seq", None),
    )
    out_specs = P(("dp", "seq"), None, None)
    return jax.shard_map(shards, mesh=mesh, in_specs=in_specs, out_specs=out_specs, check_vma=False)
```

```python
import math

import jax
import jax.numpy as jnp
from jax import lax
from jax.experimental import pallas as pl
from jax.experimental.pallas import tpu as pltpu
from jax.sharding import PartitionSpec as P

HEADS = 16
HEAD = 72
D = 1152
LANES = 128
SEQ = 32
LOCAL = 3
PATCH = 8
CAP = 120
ROWS = 256
HALF = 128
HALVES = ((0, 640), (640, D))
BF = jnp.bfloat16
F32 = jnp.float32
MESH = pl.DeviceIdType.MESH
EXP_SCALE = HEAD ** (-0.5) * math.log2(math.e)


def window(head):
    low = HEAD * head
    return low // LANES * LANES, -(-(low + HEAD) // LANES) * LANES


def dot_nt(a, b):
    return lax.dot_general(a, b, (((1,), (1,)), ((), ())), preferred_element_type=F32)


def dot_nn(a, b):
    return jnp.dot(a, b, preferred_element_type=F32)


def head_mask(head):
    first, last = window(head)
    lane = lax.broadcasted_iota(jnp.int32, (1, last - first), 1) + first
    return jnp.where((lane >= HEAD * head) & (lane < HEAD * (head + 1)), 1.0, 0.0).astype(BF)


def placed(head):
    first, last = window(head)
    shape = (HEAD, last - first)
    feature = lax.broadcasted_iota(jnp.int32, shape, 0)
    lane = lax.broadcasted_iota(jnp.int32, shape, 1) + first
    return jnp.where(lane == feature + HEAD * head, 1.0, 0.0).astype(BF)


def frame_to_patch():
    row = lax.broadcasted_iota(jnp.int32, (HALF, HALF), 0)
    column = lax.broadcasted_iota(jnp.int32, (HALF, HALF), 1)
    return jnp.where(column == (row % 16) * PATCH + row // 16, 1.0, 0.0).astype(BF)


def patch_to_frame():
    row = lax.broadcasted_iota(jnp.int32, (ROWS, ROWS), 0)
    column = lax.broadcasted_iota(jnp.int32, (ROWS, ROWS), 1)
    return jnp.where(column == (row % PATCH) * SEQ + row // PATCH, 1.0, 0.0).astype(BF)


def spans(first, last, step=512):
    return [(c, min(c + step, last)) for c in range(first, last, step)]


def attend_heads(score, value_t, store, buffers, group, allowed=None):
    scores, weights, inverse = buffers
    groups = HEADS // group

    def multiply(g):
        for i in range(group):
            scores[g % 2, i] = score(g * group + i)

    def soften(g):
        for i in range(group):
            rows = scores[g % 2, i]
            if allowed is not None:
                rows = jnp.where(allowed, rows, -1e30)
            top = jnp.max(rows, axis=0, keepdims=True)
            raised = jnp.exp2((rows - top) * EXP_SCALE)
            inverse[g % 2, i] = 1.0 / jnp.sum(raised, axis=0, keepdims=True)
            weights[g % 2, i] = raised.astype(BF)

    def mix(g):
        for i in range(group):
            store(g * group + i, dot_nn(value_t(g * group + i), weights[g % 2, i]) * inverse[g % 2, i])

    multiply(0)
    for g in range(groups):
        if g + 1 < groups:
            multiply(g + 1)
        soften(g)
        mix(g)


def landed(ref, semaphore):
    pltpu.make_async_copy(ref, ref, semaphore).wait()


def kernel(
    caption_len, frames_ref, modulation, caption_ref, wsqkv_ref, wsp_ref, wtqkv_ref, wtp_ref, wcq_ref, wco_ref,
    out_ref,
    frames, wsqkv, wsp, wtqkv, wtp, wy, wg, cap, cap_keys,
    modulated, qk, vt, mix_t, mix, sent, received, x, tqk, tv, tvt, tmix_t, tmix,
    scores, weights, inverse, tscores, tweights, tinverse, cscores, cweights, cinverse,
    load_sem, y_send, y_recv, g_send, g_recv, z_send, z_recv, s_send, s_recv, c_send, c_recv,
    f_send, f_recv, r_send, r_recv, local_sem,
):
    me = lax.axis_index("seq")
    dp = lax.axis_index("dp")
    core = dp % 2
    my_x, my_z, my_y = me // 8, (me // 4) % 2, me % 4
    other_core = dp + 1 - 2 * core
    across = (dp + 2) % 4

    def peer_of(k):
        y = (my_y + k % 4) % 4
        x_ = (my_x + (k // 4) % 4) % 4
        z = (my_z + k // 16) % 2
        return x_ * 8 + z * 4 + y

    def place_of(x_, z, y):
        return (x_ + z + y) % 2 * 16 + x_ * 4 + z * 2 + y // 2

    my_place = place_of(my_x, my_z, my_y)
    my_parity = my_place // 16

    def parity_peer(turn, n):
        k_x, k_z = n // 4, n // 2 % 2
        k_y = n % 2 * 2 + (k_x + k_z + 1 + turn) % 2
        x_, z, y = (my_x + k_x) % 4, (my_z + k_z) % 2, (my_y + k_y) % 4
        return x_ * 8 + z * 4 + y, place_of(x_, z, y)

    facing = my_x * 8 + (1 - my_z) * 4 + my_y

    barrier = pltpu.get_barrier_semaphore()

    @pl.loop(1, SEQ)
    def _(k):
        pl.semaphore_signal(barrier, inc=1, device_id={"seq": peer_of(k)}, device_id_type=MESH)

    pl.semaphore_signal(barrier, inc=1, device_id={"dp": other_core}, device_id_type=MESH)
    pl.semaphore_signal(barrier, inc=1, device_id={"dp": across, "seq": facing}, device_id_type=MESH)

    def load(i):
        source, target = [
            (frames_ref.at[0], frames.at[0]),
            (wsqkv_ref.at[:, :1024], wsqkv.at[:, :1024]),
            (wsqkv_ref.at[:, 1024 : 2 * D], wsqkv.at[:, 1024 : 2 * D]),
            (wsqkv_ref.at[:, 2 * D :], wsqkv.at[:, 2 * D :]),
            (wsp_ref, wsp),
            (frames_ref.at[pl.ds(1, 2)], frames.at[pl.ds(1, 2)]),
            (wtqkv_ref, wtqkv),
            (wtp_ref, wtp),
        ][i]
        return pltpu.make_async_copy(source, target, load_sem.at[i])

    for i in range(3):
        load(i).start()
    own_caption = pltpu.make_async_copy(caption_ref, cap.at[me], local_sem.at[0])
    own_caption.start()

    def by_core(step):
        for c in range(2):
            @pl.when(core == c)
            def _():
                step(c, slice(*HALVES[c]))

    def own_weight(m, columns):
        source = (wcq_ref, wco_ref)[m].at[:, columns]
        return pltpu.make_async_copy(source, wy.at[m, my_x * 4 + my_y, :, columns], local_sem.at[5 + m])

    def first_gather(c, columns):
        for m in range(2):
            own_weight(m, columns).start()

        for m, source in enumerate((wcq_ref, wco_ref)):
            @pl.loop(1, 4)
            def _(k):
                peer = (my_x + c * k) % 4 * 8 + my_z * 4 + (my_y + (1 - c) * k) % 4
                pltpu.make_async_remote_copy(
                    source.at[:, columns], wy.at[m, my_x * 4 + my_y, :, columns], y_send.at[m], y_recv.at[m],
                    device_id={"seq": peer}, device_id_type=MESH,
                ).start()

    def group_slot(c, i):
        return my_x * 4 + i if c == 0 else i * 4 + my_y

    def face_gather(c, columns):
        own_weight(1, columns).wait()
        landed(wy.at[1, pl.ds(0, 3), :, columns], y_recv.at[1])

        @pl.loop(0, 4)
        def _(i):
            pltpu.make_async_remote_copy(
                wy.at[1, group_slot(c, i), :, columns], wy.at[2, group_slot(c, i), :, columns],
                z_send.at[1], z_recv.at[1], device_id={"dp": across, "seq": facing}, device_id_type=MESH,
            ).start()

    def second_gather(m):
        def step(c, columns):
            if m == 0:
                own_weight(0, columns).wait()
                landed(wy.at[0, pl.ds(0, 3), :, columns], y_recv.at[0])
            else:
                landed(wy.at[2, pl.ds(0, 4), :, columns], z_recv.at[1])

            @pl.loop(0, 12 * (m + 1))
            def _(n):
                k, i = 1 + n // 4 % 3, n % 4
                block = wy.at[m + n // 12, group_slot(c, i), :, columns]
                peer = (my_x + (1 - c) * k) % 4 * 8 + my_z * 4 + (my_y + c * k) % 4
                pltpu.make_async_remote_copy(
                    block, block, g_send.at[m], g_recv.at[m], device_id={"seq": peer}, device_id_type=MESH
                ).start()

        by_core(step)

    def swap(m, block, half, columns):
        part = wg.at[m, block, :, columns]
        return pltpu.make_async_remote_copy(
            part, part, s_send.at[m, half], s_recv.at[m, half], device_id={"dp": other_core}, device_id_type=MESH
        )

    def third_gather(m):
        def step(c, columns):
            landed(wy.at[pl.ds(m, m + 1), pl.ds(0, 12), :, columns], g_recv.at[m])
            for plane in range(m, 2 * m + 1):
                for group in range(4):
                    block = group * 2 + (my_z if plane == m else 1 - my_z)
                    for y in range(4):
                        wg[m, block, 36 * y : 36 * (y + 1), columns] = wy[plane, group * 4 + y, :, columns]
            for group in range(4):
                if m == 0:
                    block = wg.at[0, group * 2 + my_z, :, columns]
                    pltpu.make_async_remote_copy(
                        block, block, z_send.at[0], z_recv.at[0],
                        device_id={"dp": across, "seq": facing}, device_id_type=MESH,
                    ).start()
                else:
                    swap(1, group * 2 + 1 - my_z, 1, columns).start()
                swap(m, group * 2 + my_z, 0, columns).start()

        by_core(step)

    def last_gather(c, columns):
        landed(wg.at[0, pl.ds(0, 4), :, columns], z_recv.at[0])
        for group in range(4):
            swap(0, group * 2 + 1 - my_z, 1, columns).start()

    def whole_weight(m):
        def step(c, columns):
            for half in range(2):
                landed(wg.at[m, pl.ds(0, 4), :, slice(*HALVES[1 - c])], s_recv.at[m, half])

        by_core(step)

    def sent_weights(c, columns):
        landed(wg.at[0, pl.ds(0, 4), :, columns], z_send.at[0])
        landed(wy.at[2, pl.ds(0, 4), :, columns], z_send.at[1])
        for m in range(2):
            landed(wy.at[m, pl.ds(0, 3), :, columns], y_send.at[m])
            landed(wy.at[pl.ds(m, m + 1), pl.ds(0, 12), :, columns], g_send.at[m])
            for half in range(2):
                landed(wg.at[m, pl.ds(0, 4), :, columns], s_send.at[m, half])

    pl.semaphore_wait(barrier, SEQ + 1)

    by_core(first_gather)

    def spatial(f, _):
        @pl.when(f == 0)
        def _():
            load(0).wait()

        @pl.when(f == 1)
        def _():
            load(5).wait()

        @pl.loop(0, ROWS // 32, unroll=8)
        def _(r):
            rows = pl.ds(pl.multiple_of(r * 32, 32), 32)
            wide = frames[f, rows, :].astype(F32)
            centered = wide - jnp.mean(wide, axis=-1, keepdims=True)
            variance = jnp.mean(centered * centered, axis=-1, keepdims=True)
            normed = centered * lax.rsqrt(variance + 1e-06)
            modulated[rows, :] = (normed * (1.0 + modulation[1:2, :]) + modulation[0:1, :]).astype(BF)

        @pl.when(f == 0)
        def _():
            load(1).wait()
            load(3).start()
            load(4).start()

        for first, last in spans(0, 1024):
            qk[:, first:last] = dot_nn(modulated[...], wsqkv[:, first:last]).astype(BF)

        @pl.when(f == 0)
        def _():
            load(2).wait()
            load(5).start()
            second_gather(0)
            by_core(face_gather)

        for first, last in spans(1024, 2 * D):
            qk[:, first:last] = dot_nn(modulated[...], wsqkv[:, first:last]).astype(BF)

        @pl.when(f == 0)
        def _():
            load(3).wait()
            load(6).start()

        for first, last in spans(0, D):
            vt[first:last, :] = dot_nn(modulated[...], wsqkv[:, 2 * D + first : 2 * D + last]).T

        def score(head):
            first, last = window(head)
            return dot_nt(qk[:, D + first : D + last] * head_mask(head), qk[:, first:last])

        def store(head, rows):
            mix_t[HEAD * head : HEAD * (head + 1), :] = rows

        attend_heads(
            score, lambda head: vt[HEAD * head : HEAD * (head + 1), :].astype(BF), store, (scores, weights, inverse), 4
        )
        for first, last in spans(0, D):
            mix[:, first:last] = mix_t[first:last, :].T.astype(BF)

        @pl.when(f == 1)
        def _():
            third_gather(0)

        @pl.when(f == 0)
        def _():
            load(4).wait()
            load(7).start()

        for first, last in spans(0, D):
            branch = dot_nn(mix[...], wsp[:, first:last])
            after = frames[f, :, first:last].astype(F32) + modulation[2:3, first:last] * branch
            sent[f, :, :, first:last] = after.reshape(SEQ, PATCH, last - first).astype(BF)

        for turn in range(2):
            @pl.loop(turn, 16)
            def _(n):
                peer, _ = parity_peer(turn, n)
                pltpu.make_async_remote_copy(
                    sent.at[f, peer], received.at[f, my_place], f_send.at[f], f_recv.at[f, turn],
                    device_id={"seq": peer}, device_id_type=MESH,
                ).start()

        received[f, my_place] = sent[f, me]
        return 0

    lax.fori_loop(0, LOCAL, spatial, 0)
    second_gather(1)

    @pl.loop(1, SEQ)
    def _(k):
        pltpu.make_async_remote_copy(
            caption_ref, cap.at[me], c_send, c_recv, device_id={"seq": peer_of(k)}, device_id_type=MESH
        ).start()

    order = frame_to_patch()

    @pl.loop(0, LOCAL)
    def _(f):
        for turn in range(2):
            landed(received.at[f, pl.ds(0, 16 - turn)], f_recv.at[f, turn])

            if turn == 0:
                @pl.when(f == 0)
                def _():
                    load(6).wait()

            first_place = pl.multiple_of((my_parity + 1 + turn) % 2 * 16, 16)
            places = pl.ds(first_place, 16)
            for first, last in spans(0, D):
                block = received[f, places, :, first:last].astype(F32).reshape(HALF, last - first).astype(BF)
                block = dot_nn(order, block).astype(BF)
                modulated[:HALF, first:last] = block
                x[f, :, places, first:last] = block.reshape(PATCH, 16, last - first)
            frame_rows = pl.ds(pl.multiple_of(f * SEQ + first_place, 16), 16)
            for first, last in spans(0, 2 * D):
                product = dot_nn(modulated[:HALF, :], wtqkv[:, first:last]).astype(BF)
                tqk[:, frame_rows, first:last] = product.reshape(PATCH, 16, last - first)
            for first, last in spans(0, D):
                product = dot_nn(modulated[:HALF, :], wtqkv[:, 2 * D + first : 2 * D + last]).astype(BF)
                tv[:, frame_rows, first:last] = product.reshape(PATCH, 16, last - first)

    by_core(last_gather)

    frames_all = LOCAL * SEQ

    def temporal(p, _):
        for first, last in spans(0, D, 384):
            tvt[first:last, :] = tv[p, :, first:last].astype(F32).T

        def score(head):
            first, last = window(head)
            return dot_nt(tqk[p, :, D + first : D + last] * head_mask(head), tqk[p, :, first:last])

        def store(head, rows):
            tmix_t[HEAD * head : HEAD * (head + 1), :frames_all] = rows

        attend_heads(
            score, lambda head: tvt[HEAD * head : HEAD * (head + 1), :frames_all].astype(BF), store,
            (tscores, tweights, tinverse), 8,
        )
        for first, last in spans(0, D, 384):
            block = tmix_t[first:last, :].T.astype(BF)
            for f in range(LOCAL):
                tmix[f, p, :, first:last] = block[f * SEQ : (f + 1) * SEQ]
        return 0

    tv[:, frames_all:, :] = jnp.zeros((PATCH, LANES - frames_all, D), BF)
    tmix_t[...] = jnp.zeros((D, LANES), F32)
    lax.fori_loop(0, PATCH, temporal, 0)
    third_gather(1)

    load(7).wait()
    for f in range(LOCAL):
        landed(sent.at[f, pl.ds(0, SEQ - 1)], f_send.at[f])

    def finish(f, _):
        after = modulated
        for first, last in spans(0, D):
            branch = dot_nn(tmix[f].reshape(ROWS, D), wtp[:, first:last])
            after[:, first:last] = (
                x[f, :, :, first:last].reshape(ROWS, last - first).astype(F32) + modulation[2:3, first:last] * branch
            ).astype(BF)

        @pl.when(f == 0)
        def _():
            whole_weight(0)

        for first, last in spans(0, D):
            qk[:, first:last] = dot_nn(after[...], wg[0, :, :, first:last].reshape(D, last - first)).astype(BF)

        @pl.when(f == 0)
        def _():
            own_caption.wait()
            landed(cap.at[pl.ds(0, SEQ - 1)], c_recv)
            for head in range(HEADS):
                first, last = window(head)
                cap_keys[head, :, : last - first] = lax.dot_general(
                    cap[head], placed(head), (((0,), (0,)), ((), ())), preferred_element_type=F32
                ).astype(BF)

        def score(head):
            first, last = window(head)
            return dot_nt(cap_keys[head, :, : last - first], qk[:, first:last])

        def store(head, rows):
            mix_t[HEAD * head : HEAD * (head + 1), :] = rows

        allowed = lax.broadcasted_iota(jnp.int32, (CAP, ROWS), 0) < caption_len[0]
        attend_heads(score, lambda head: cap[HEADS + head], store, (cscores, cweights, cinverse), 4, allowed)
        for first, last in spans(0, D):
            mix[:, first:last] = mix_t[first:last, :].T.astype(BF)

        @pl.when(f == 0)
        def _():
            whole_weight(1)

        order = patch_to_frame()
        for first, last in spans(0, D):
            branch = dot_nn(mix[...], wg[1, :, :, first:last].reshape(D, last - first))
            rows = (after[:, first:last].astype(F32) + branch).astype(BF)
            sent[f, :, :, first:last] = dot_nn(order, rows).reshape(SEQ, PATCH, last - first).astype(BF)

        @pl.loop(1, SEQ)
        def _(k):
            y = (my_y + k % 4) % 4
            x_ = (my_x + k // 4 % 4) % 4
            z = (my_z + k // 16) % 2
            pltpu.make_async_remote_copy(
                sent.at[f, place_of(x_, z, y)], out_ref.at[f, me], r_send.at[f], r_recv.at[f],
                device_id={"seq": x_ * 8 + z * 4 + y}, device_id_type=MESH,
            ).start()

        pltpu.make_async_copy(sent.at[f, my_place], out_ref.at[f, me], local_sem.at[2 + f]).start()
        return 0

    lax.fori_loop(0, LOCAL, finish, 0)

    for f in range(LOCAL):
        pltpu.make_async_copy(sent.at[f, my_place], out_ref.at[f, me], local_sem.at[2 + f]).wait()
        landed(sent.at[f, pl.ds(0, SEQ - 1)], r_send.at[f])
        landed(out_ref.at[f, pl.ds(0, SEQ - 1)], r_recv.at[f])
    by_core(sent_weights)
    landed(cap.at[pl.ds(0, SEQ - 1)], c_send)


def shards(
    frames_in, modulation, caption_kv, caption_len,
    w_spatial_qkv, w_spatial_proj, w_temporal_qkv, w_temporal_proj, w_cross_q, w_cross_out,
):
    vmem = pl.BlockSpec(memory_space=pltpu.VMEM)
    whole = pl.BlockSpec(memory_space=pl.ANY)
    dma = pltpu.SemaphoreType.DMA
    out = pl.pallas_call(
        kernel,
        out_shape=pltpu.VMEM((LOCAL, SEQ, PATCH, D), BF),
        in_specs=[pl.BlockSpec(memory_space=pltpu.SMEM), whole, vmem] + [whole] * 7,
        out_specs=whole,
        scratch_shapes=[
            pltpu.VMEM((LOCAL, ROWS, D), BF),
            pltpu.VMEM((D, 3 * D), BF),
            pltpu.VMEM((D, D), BF),
            pltpu.VMEM((D, 3 * D), BF),
            pltpu.VMEM((D, D), BF),
            pltpu.VMEM((3, 16, 36, D), BF),
            pltpu.VMEM((2, 8, 144, D), BF),
            pltpu.VMEM((SEQ, HEAD, CAP), BF),
            pltpu.VMEM((HEADS, CAP, 2 * LANES), BF),
            pltpu.VMEM((ROWS, D), BF),
            pltpu.VMEM((ROWS, 2 * D), BF),
            pltpu.VMEM((D, ROWS), F32),
            pltpu.VMEM((D, ROWS), F32),
            pltpu.VMEM((ROWS, D), BF),
            pltpu.VMEM((LOCAL, SEQ, PATCH, D), BF),
            pltpu.VMEM((LOCAL, SEQ, PATCH, D), BF),
            pltpu.VMEM((LOCAL, PATCH, SEQ, D), BF),
            pltpu.VMEM((PATCH, LOCAL * SEQ, 2 * D), BF),
            pltpu.VMEM((PATCH, LANES, D), BF),
            pltpu.VMEM((D, LANES), F32),
            pltpu.VMEM((D, LANES), F32),
            pltpu.VMEM((LOCAL, PATCH, SEQ, D), BF),
            pltpu.VMEM((2, 4, ROWS, ROWS), F32),
            pltpu.VMEM((2, 4, ROWS, ROWS), BF),
            pltpu.VMEM((2, 4, 1, ROWS), F32),
            pltpu.VMEM((2, 8, LOCAL * SEQ, LOCAL * SEQ), F32),
            pltpu.VMEM((2, 8, LOCAL * SEQ, LOCAL * SEQ), BF),
            pltpu.VMEM((2, 8, 1, LOCAL * SEQ), F32),
            pltpu.VMEM((2, 4, CAP, ROWS), F32),
            pltpu.VMEM((2, 4, CAP, ROWS), BF),
            pltpu.VMEM((2, 4, 1, ROWS), F32),
            dma((8,)),
            dma((2,)), dma((2,)), dma((2,)), dma((2,)), dma((2,)), dma((2,)), dma((2, 2)), dma((2, 2)), dma, dma,
            dma((LOCAL,)), dma((LOCAL, 2)), dma((LOCAL,)), dma((LOCAL,)),
            dma((7,)),
        ],
        compiler_params=pltpu.CompilerParams(
            collective_id=0, has_side_effects=True, vmem_limit_bytes=60 * 1024 * 1024
        ),
        name="block",
    )(
        caption_len, frames_in, modulation, caption_kv.T,
        w_spatial_qkv, w_spatial_proj, w_temporal_qkv, w_temporal_proj, w_cross_q, w_cross_out,
    )
    return out.reshape(frames_in.shape)


def solution(mesh):
    in_specs = (
        P(("dp", "seq"), None, None),
        P("dp", None),
        P("dp", "seq"),
        P("dp"),
        P(),
        P(),
        P(),
        P(),
        P("seq", None),
        P("seq", None),
    )
    out_specs = P(("dp", "seq"), None, None)
    return jax.shard_map(shards, mesh=mesh, in_specs=in_specs, out_specs=out_specs, check_vma=False)
```

```python
import math

import jax
import jax.numpy as jnp
from jax import lax
from jax.experimental import pallas as pl
from jax.experimental.pallas import tpu as pltpu
from jax.sharding import PartitionSpec as P

HEADS = 16
HEAD = 72
D = 1152
LANES = 128
SEQ = 32
LOCAL = 3
PATCH = 8
CAP = 120
ROWS = 256
HALF = 128
HALVES = ((0, 640), (640, D))
BF = jnp.bfloat16
F32 = jnp.float32
MESH = pl.DeviceIdType.MESH
EXP_SCALE = HEAD ** (-0.5) * math.log2(math.e)


def window(head):
    low = HEAD * head
    return low // LANES * LANES, -(-(low + HEAD) // LANES) * LANES


def dot_nt(a, b):
    return lax.dot_general(a, b, (((1,), (1,)), ((), ())), preferred_element_type=F32)


def dot_nn(a, b):
    return jnp.dot(a, b, preferred_element_type=F32)


def head_mask(head):
    first, last = window(head)
    lane = lax.broadcasted_iota(jnp.int32, (1, last - first), 1) + first
    return jnp.where((lane >= HEAD * head) & (lane < HEAD * (head + 1)), 1.0, 0.0).astype(BF)


def placed(head):
    first, last = window(head)
    shape = (HEAD, last - first)
    feature = lax.broadcasted_iota(jnp.int32, shape, 0)
    lane = lax.broadcasted_iota(jnp.int32, shape, 1) + first
    return jnp.where(lane == feature + HEAD * head, 1.0, 0.0).astype(BF)


def frame_to_patch():
    row = lax.broadcasted_iota(jnp.int32, (HALF, HALF), 0)
    column = lax.broadcasted_iota(jnp.int32, (HALF, HALF), 1)
    return jnp.where(column == (row % 16) * PATCH + row // 16, 1.0, 0.0).astype(BF)


def patch_to_frame():
    row = lax.broadcasted_iota(jnp.int32, (ROWS, ROWS), 0)
    column = lax.broadcasted_iota(jnp.int32, (ROWS, ROWS), 1)
    return jnp.where(column == (row % PATCH) * SEQ + row // PATCH, 1.0, 0.0).astype(BF)


def spans(first, last, step=512):
    return [(c, min(c + step, last)) for c in range(first, last, step)]


def attend_heads(score, value_t, store, buffers, group, allowed=None):
    scores, weights, inverse = buffers
    groups = HEADS // group

    def multiply(g):
        for i in range(group):
            scores[g % 2, i] = score(g * group + i)

    def soften(g):
        for i in range(group):
            rows = scores[g % 2, i]
            if allowed is not None:
                rows = jnp.where(allowed, rows, -1e30)
            top = jnp.max(rows, axis=0, keepdims=True)
            raised = jnp.exp2((rows - top) * EXP_SCALE)
            inverse[g % 2, i] = 1.0 / jnp.sum(raised, axis=0, keepdims=True)
            weights[g % 2, i] = raised.astype(BF)

    def mix(g):
        for i in range(group):
            store(g * group + i, dot_nn(value_t(g * group + i), weights[g % 2, i]) * inverse[g % 2, i])

    multiply(0)
    for g in range(groups):
        if g + 1 < groups:
            multiply(g + 1)
        soften(g)
        mix(g)


def landed(ref, semaphore):
    pltpu.make_async_copy(ref, ref, semaphore).wait()


def kernel(
    caption_len, frames_ref, modulation, caption_ref, wsqkv_ref, wsp_ref, wtqkv_ref, wtp_ref, wcq_ref, wco_ref,
    out_ref,
    frames, wsqkv, wsp, wtqkv, wtp, wy, wg, cap, cap_keys,
    modulated, qk, vt, mix_t, mix, sent, received, x, tqk, tv, tvt, tmix_t, tmix,
    scores, weights, inverse, tscores, tweights, tinverse, cscores, cweights, cinverse,
    load_sem, y_send, y_recv, g_send, g_recv, z_send, z_recv, s_send, s_recv, c_send, c_recv,
    f_send, f_recv, r_send, r_recv, local_sem,
):
    me = lax.axis_index("seq")
    dp = lax.axis_index("dp")
    core = dp % 2
    my_x, my_z, my_y = me // 8, (me // 4) % 2, me % 4
    other_core = dp + 1 - 2 * core
    across = (dp + 2) % 4

    def peer_of(k):
        y = (my_y + k % 4) % 4
        x_ = (my_x + (k // 4) % 4) % 4
        z = (my_z + k // 16) % 2
        return x_ * 8 + z * 4 + y

    def place_of(x_, z, y):
        return (x_ + z + y) % 2 * 16 + x_ * 4 + z * 2 + y // 2

    my_place = place_of(my_x, my_z, my_y)
    my_parity = my_place // 16

    def parity_peer(turn, n):
        k_x, k_z = n // 4, n // 2 % 2
        k_y = n % 2 * 2 + (k_x + k_z + 1 + turn) % 2
        x_, z, y = (my_x + k_x) % 4, (my_z + k_z) % 2, (my_y + k_y) % 4
        return x_ * 8 + z * 4 + y, place_of(x_, z, y)

    facing = my_x * 8 + (1 - my_z) * 4 + my_y

    barrier = pltpu.get_barrier_semaphore()

    @pl.loop(1, SEQ)
    def _(k):
        pl.semaphore_signal(barrier, inc=1, device_id={"seq": peer_of(k)}, device_id_type=MESH)

    pl.semaphore_signal(barrier, inc=1, device_id={"dp": other_core}, device_id_type=MESH)
    pl.semaphore_signal(barrier, inc=1, device_id={"dp": across, "seq": facing}, device_id_type=MESH)

    def load(i):
        source, target = [
            (frames_ref.at[0], frames.at[0]),
            (wsqkv_ref.at[:, :1024], wsqkv.at[:, :1024]),
            (wsqkv_ref.at[:, 1024 : 2 * D], wsqkv.at[:, 1024 : 2 * D]),
            (wsqkv_ref.at[:, 2 * D :], wsqkv.at[:, 2 * D :]),
            (wsp_ref, wsp),
            (frames_ref.at[pl.ds(1, 2)], frames.at[pl.ds(1, 2)]),
            (wtqkv_ref, wtqkv),
            (wtp_ref, wtp),
        ][i]
        return pltpu.make_async_copy(source, target, load_sem.at[i])

    for i in range(3):
        load(i).start()
    own_caption = pltpu.make_async_copy(caption_ref, cap.at[me], local_sem.at[0])
    own_caption.start()

    def by_core(step):
        for c in range(2):
            @pl.when(core == c)
            def _():
                step(c, slice(*HALVES[c]))

    def own_weight(m, columns):
        source = (wcq_ref, wco_ref)[m].at[:, columns]
        return pltpu.make_async_copy(source, wy.at[m, my_x * 4 + my_y, :, columns], local_sem.at[5 + m])

    def first_gather(c, columns):
        for m in range(2):
            own_weight(m, columns).start()

        for m, source in enumerate((wcq_ref, wco_ref)):
            @pl.loop(1, 4)
            def _(k):
                peer = (my_x + c * k) % 4 * 8 + my_z * 4 + (my_y + (1 - c) * k) % 4
                pltpu.make_async_remote_copy(
                    source.at[:, columns], wy.at[m, my_x * 4 + my_y, :, columns], y_send.at[m], y_recv.at[m],
                    device_id={"seq": peer}, device_id_type=MESH,
                ).start()

    def group_slot(c, i):
        return my_x * 4 + i if c == 0 else i * 4 + my_y

    def face_gather(c, columns):
        own_weight(1, columns).wait()
        landed(wy.at[1, pl.ds(0, 3), :, columns], y_recv.at[1])

        @pl.loop(0, 4)
        def _(i):
            pltpu.make_async_remote_copy(
                wy.at[1, group_slot(c, i), :, columns], wy.at[2, group_slot(c, i), :, columns],
                z_send.at[1], z_recv.at[1], device_id={"dp": across, "seq": facing}, device_id_type=MESH,
            ).start()

    def second_gather(m):
        def step(c, columns):
            if m == 0:
                own_weight(0, columns).wait()
                landed(wy.at[0, pl.ds(0, 3), :, columns], y_recv.at[0])
            else:
                landed(wy.at[2, pl.ds(0, 4), :, columns], z_recv.at[1])

            @pl.loop(0, 12 * (m + 1))
            def _(n):
                k, i = 1 + n // 4 % 3, n % 4
                block = wy.at[m + n // 12, group_slot(c, i), :, columns]
                peer = (my_x + (1 - c) * k) % 4 * 8 + my_z * 4 + (my_y + c * k) % 4
                pltpu.make_async_remote_copy(
                    block, block, g_send.at[m], g_recv.at[m], device_id={"seq": peer}, device_id_type=MESH
                ).start()

        by_core(step)

    def swap(m, block, half, columns):
        part = wg.at[m, block, :, columns]
        return pltpu.make_async_remote_copy(
            part, part, s_send.at[m, half], s_recv.at[m, half], device_id={"dp": other_core}, device_id_type=MESH
        )

    def third_gather(m):
        def step(c, columns):
            landed(wy.at[pl.ds(m, m + 1), pl.ds(0, 12), :, columns], g_recv.at[m])
            for plane in range(m, 2 * m + 1):
                for group in range(4):
                    block = group * 2 + (my_z if plane == m else 1 - my_z)
                    for y in range(4):
                        wg[m, block, 36 * y : 36 * (y + 1), columns] = wy[plane, group * 4 + y, :, columns]
            for group in range(4):
                if m == 0:
                    block = wg.at[0, group * 2 + my_z, :, columns]
                    pltpu.make_async_remote_copy(
                        block, block, z_send.at[0], z_recv.at[0],
                        device_id={"dp": across, "seq": facing}, device_id_type=MESH,
                    ).start()
                else:
                    swap(1, group * 2 + 1 - my_z, 1, columns).start()
                swap(m, group * 2 + my_z, 0, columns).start()

        by_core(step)

    def last_gather(c, columns):
        landed(wg.at[0, pl.ds(0, 4), :, columns], z_recv.at[0])
        for group in range(4):
            swap(0, group * 2 + 1 - my_z, 1, columns).start()

    def whole_weight(m):
        def step(c, columns):
            for half in range(2):
                landed(wg.at[m, pl.ds(0, 4), :, slice(*HALVES[1 - c])], s_recv.at[m, half])

        by_core(step)

    def sent_weights(c, columns):
        landed(wg.at[0, pl.ds(0, 4), :, columns], z_send.at[0])
        landed(wy.at[2, pl.ds(0, 4), :, columns], z_send.at[1])
        for m in range(2):
            landed(wy.at[m, pl.ds(0, 3), :, columns], y_send.at[m])
            landed(wy.at[pl.ds(m, m + 1), pl.ds(0, 12), :, columns], g_send.at[m])
            for half in range(2):
                landed(wg.at[m, pl.ds(0, 4), :, columns], s_send.at[m, half])

    pl.semaphore_wait(barrier, SEQ + 1)

    by_core(first_gather)

    def spatial(f, _):
        @pl.when(f == 0)
        def _():
            load(0).wait()

        @pl.when(f == 1)
        def _():
            load(5).wait()

        @pl.loop(0, ROWS // 32, unroll=8)
        def _(r):
            rows = pl.ds(pl.multiple_of(r * 32, 32), 32)
            wide = frames[f, rows, :].astype(F32)
            centered = wide - jnp.mean(wide, axis=-1, keepdims=True)
            variance = jnp.mean(centered * centered, axis=-1, keepdims=True)
            normed = centered * lax.rsqrt(variance + 1e-06)
            modulated[rows, :] = (normed * (1.0 + modulation[1:2, :]) + modulation[0:1, :]).astype(BF)

        @pl.when(f == 0)
        def _():
            load(1).wait()
            load(3).start()
            load(4).start()

        for first, last in spans(0, 1024):
            qk[:, first:last] = dot_nn(modulated[...], wsqkv[:, first:last]).astype(BF)

        @pl.when(f == 0)
        def _():
            load(2).wait()
            load(5).start()
            second_gather(0)
            by_core(face_gather)

        for first, last in spans(1024, 2 * D):
            qk[:, first:last] = dot_nn(modulated[...], wsqkv[:, first:last]).astype(BF)

        @pl.when(f == 0)
        def _():
            load(3).wait()
            load(6).start()

        for first, last in spans(0, D):
            vt[first:last, :] = dot_nn(modulated[...], wsqkv[:, 2 * D + first : 2 * D + last]).T

        def score(head):
            first, last = window(head)
            return dot_nt(qk[:, D + first : D + last] * head_mask(head), qk[:, first:last])

        def store(head, rows):
            mix_t[HEAD * head : HEAD * (head + 1), :] = rows

        attend_heads(
            score, lambda head: vt[HEAD * head : HEAD * (head + 1), :].astype(BF), store, (scores, weights, inverse), 4
        )
        for first, last in spans(0, D):
            mix[:, first:last] = mix_t[first:last, :].T.astype(BF)

        @pl.when(f == 1)
        def _():
            third_gather(0)

        @pl.when(f == 0)
        def _():
            load(4).wait()
            load(7).start()

        for first, last in spans(0, D):
            branch = dot_nn(mix[...], wsp[:, first:last])
            after = frames[f, :, first:last].astype(F32) + modulation[2:3, first:last] * branch
            sent[f, :, :, first:last] = after.reshape(SEQ, PATCH, last - first).astype(BF)

        for turn in range(2):
            @pl.loop(turn, 16)
            def _(n):
                peer, _ = parity_peer(turn, n)
                pltpu.make_async_remote_copy(
                    sent.at[f, peer], received.at[f, my_place], f_send.at[f], f_recv.at[f, turn],
                    device_id={"seq": peer}, device_id_type=MESH,
                ).start()

        received[f, my_place] = sent[f, me]
        return 0

    lax.fori_loop(0, LOCAL, spatial, 0)
    second_gather(1)

    @pl.loop(1, SEQ)
    def _(k):
        pltpu.make_async_remote_copy(
            caption_ref, cap.at[me], c_send, c_recv, device_id={"seq": peer_of(k)}, device_id_type=MESH
        ).start()

    order = frame_to_patch()

    @pl.loop(0, LOCAL)
    def _(f):
        for turn in range(2):
            landed(received.at[f, pl.ds(0, 16 - turn)], f_recv.at[f, turn])

            if turn == 0:
                @pl.when(f == 0)
                def _():
                    load(6).wait()

            first_place = pl.multiple_of((my_parity + 1 + turn) % 2 * 16, 16)
            places = pl.ds(first_place, 16)
            for first, last in spans(0, D):
                block = received[f, places, :, first:last].astype(F32).reshape(HALF, last - first).astype(BF)
                block = dot_nn(order, block).astype(BF)
                modulated[:HALF, first:last] = block
                x[f, :, places, first:last] = block.reshape(PATCH, 16, last - first)
            frame_rows = pl.ds(pl.multiple_of(f * SEQ + first_place, 16), 16)
            for first, last in spans(0, 2 * D):
                product = dot_nn(modulated[:HALF, :], wtqkv[:, first:last]).astype(BF)
                tqk[:, frame_rows, first:last] = product.reshape(PATCH, 16, last - first)
            for first, last in spans(0, D):
                product = dot_nn(modulated[:HALF, :], wtqkv[:, 2 * D + first : 2 * D + last]).astype(BF)
                tv[:, frame_rows, first:last] = product.reshape(PATCH, 16, last - first)

    by_core(last_gather)

    frames_all = LOCAL * SEQ

    def temporal(p, _):
        for first, last in spans(0, D, 384):
            tvt[first:last, :] = tv[p, :, first:last].astype(F32).T

        def score(head):
            first, last = window(head)
            return dot_nt(tqk[p, :, D + first : D + last] * head_mask(head), tqk[p, :, first:last])

        def store(head, rows):
            tmix_t[HEAD * head : HEAD * (head + 1), :frames_all] = rows

        attend_heads(
            score, lambda head: tvt[HEAD * head : HEAD * (head + 1), :frames_all].astype(BF), store,
            (tscores, tweights, tinverse), 8,
        )
        for first, last in spans(0, D, 384):
            block = tmix_t[first:last, :].T.astype(BF)
            for f in range(LOCAL):
                tmix[f, p, :, first:last] = block[f * SEQ : (f + 1) * SEQ]
        return 0

    tv[:, frames_all:, :] = jnp.zeros((PATCH, LANES - frames_all, D), BF)
    tmix_t[...] = jnp.zeros((D, LANES), F32)
    lax.fori_loop(0, PATCH, temporal, 0, unroll=2)
    third_gather(1)

    load(7).wait()
    for f in range(LOCAL):
        landed(sent.at[f, pl.ds(0, SEQ - 1)], f_send.at[f])

    def finish(f, _):
        after = modulated
        for first, last in spans(0, D):
            branch = dot_nn(tmix[f].reshape(ROWS, D), wtp[:, first:last])
            after[:, first:last] = (
                x[f, :, :, first:last].reshape(ROWS, last - first).astype(F32) + modulation[2:3, first:last] * branch
            ).astype(BF)

        @pl.when(f == 0)
        def _():
            whole_weight(0)

        for first, last in spans(0, D):
            qk[:, first:last] = dot_nn(after[...], wg[0, :, :, first:last].reshape(D, last - first)).astype(BF)

        @pl.when(f == 0)
        def _():
            own_caption.wait()
            landed(cap.at[pl.ds(0, SEQ - 1)], c_recv)
            for head in range(HEADS):
                first, last = window(head)
                cap_keys[head, :, : last - first] = lax.dot_general(
                    cap[head], placed(head), (((0,), (0,)), ((), ())), preferred_element_type=F32
                ).astype(BF)

        def score(head):
            first, last = window(head)
            return dot_nt(cap_keys[head, :, : last - first], qk[:, first:last])

        def store(head, rows):
            mix_t[HEAD * head : HEAD * (head + 1), :] = rows

        allowed = lax.broadcasted_iota(jnp.int32, (CAP, ROWS), 0) < caption_len[0]
        attend_heads(score, lambda head: cap[HEADS + head], store, (cscores, cweights, cinverse), 4, allowed)
        for first, last in spans(0, D):
            mix[:, first:last] = mix_t[first:last, :].T.astype(BF)

        @pl.when(f == 0)
        def _():
            whole_weight(1)

        order = patch_to_frame()
        for first, last in spans(0, D):
            branch = dot_nn(mix[...], wg[1, :, :, first:last].reshape(D, last - first))
            rows = (after[:, first:last].astype(F32) + branch).astype(BF)
            sent[f, :, :, first:last] = dot_nn(order, rows).reshape(SEQ, PATCH, last - first).astype(BF)

        @pl.loop(1, SEQ)
        def _(k):
            y = (my_y + k % 4) % 4
            x_ = (my_x + k // 4 % 4) % 4
            z = (my_z + k // 16) % 2
            pltpu.make_async_remote_copy(
                sent.at[f, place_of(x_, z, y)], out_ref.at[f, me], r_send.at[f], r_recv.at[f],
                device_id={"seq": x_ * 8 + z * 4 + y}, device_id_type=MESH,
            ).start()

        pltpu.make_async_copy(sent.at[f, my_place], out_ref.at[f, me], local_sem.at[2 + f]).start()
        return 0

    lax.fori_loop(0, LOCAL, finish, 0)

    for f in range(LOCAL):
        pltpu.make_async_copy(sent.at[f, my_place], out_ref.at[f, me], local_sem.at[2 + f]).wait()
        landed(sent.at[f, pl.ds(0, SEQ - 1)], r_send.at[f])
        landed(out_ref.at[f, pl.ds(0, SEQ - 1)], r_recv.at[f])
    by_core(sent_weights)
    landed(cap.at[pl.ds(0, SEQ - 1)], c_send)


def shards(
    frames_in, modulation, caption_kv, caption_len,
    w_spatial_qkv, w_spatial_proj, w_temporal_qkv, w_temporal_proj, w_cross_q, w_cross_out,
):
    vmem = pl.BlockSpec(memory_space=pltpu.VMEM)
    whole = pl.BlockSpec(memory_space=pl.ANY)
    dma = pltpu.SemaphoreType.DMA
    out = pl.pallas_call(
        kernel,
        out_shape=pltpu.VMEM((LOCAL, SEQ, PATCH, D), BF),
        in_specs=[pl.BlockSpec(memory_space=pltpu.SMEM), whole, vmem] + [whole] * 7,
        out_specs=whole,
        scratch_shapes=[
            pltpu.VMEM((LOCAL, ROWS, D), BF),
            pltpu.VMEM((D, 3 * D), BF),
            pltpu.VMEM((D, D), BF),
            pltpu.VMEM((D, 3 * D), BF),
            pltpu.VMEM((D, D), BF),
            pltpu.VMEM((3, 16, 36, D), BF),
            pltpu.VMEM((2, 8, 144, D), BF),
            pltpu.VMEM((SEQ, HEAD, CAP), BF),
            pltpu.VMEM((HEADS, CAP, 2 * LANES), BF),
            pltpu.VMEM((ROWS, D), BF),
            pltpu.VMEM((ROWS, 2 * D), BF),
            pltpu.VMEM((D, ROWS), F32),
            pltpu.VMEM((D, ROWS), F32),
            pltpu.VMEM((ROWS, D), BF),
            pltpu.VMEM((LOCAL, SEQ, PATCH, D), BF),
            pltpu.VMEM((LOCAL, SEQ, PATCH, D), BF),
            pltpu.VMEM((LOCAL, PATCH, SEQ, D), BF),
            pltpu.VMEM((PATCH, LOCAL * SEQ, 2 * D), BF),
            pltpu.VMEM((PATCH, LANES, D), BF),
            pltpu.VMEM((D, LANES), F32),
            pltpu.VMEM((D, LANES), F32),
            pltpu.VMEM((LOCAL, PATCH, SEQ, D), BF),
            pltpu.VMEM((2, 4, ROWS, ROWS), F32),
            pltpu.VMEM((2, 4, ROWS, ROWS), BF),
            pltpu.VMEM((2, 4, 1, ROWS), F32),
            pltpu.VMEM((2, 8, LOCAL * SEQ, LOCAL * SEQ), F32),
            pltpu.VMEM((2, 8, LOCAL * SEQ, LOCAL * SEQ), BF),
            pltpu.VMEM((2, 8, 1, LOCAL * SEQ), F32),
            pltpu.VMEM((2, 4, CAP, ROWS), F32),
            pltpu.VMEM((2, 4, CAP, ROWS), BF),
            pltpu.VMEM((2, 4, 1, ROWS), F32),
            dma((8,)),
            dma((2,)), dma((2,)), dma((2,)), dma((2,)), dma((2,)), dma((2,)), dma((2, 2)), dma((2, 2)), dma, dma,
            dma((LOCAL,)), dma((LOCAL, 2)), dma((LOCAL,)), dma((LOCAL,)),
            dma((7,)),
        ],
        compiler_params=pltpu.CompilerParams(
            collective_id=0, has_side_effects=True, vmem_limit_bytes=60 * 1024 * 1024
        ),
        name="block",
    )(
        caption_len, frames_in, modulation, caption_kv.T,
        w_spatial_qkv, w_spatial_proj, w_temporal_qkv, w_temporal_proj, w_cross_q, w_cross_out,
    )
    return out.reshape(frames_in.shape)


def solution(mesh):
    in_specs = (
        P(("dp", "seq"), None, None),
        P("dp", None),
        P("dp", "seq"),
        P("dp"),
        P(),
        P(),
        P(),
        P(),
        P("seq", None),
        P("seq", None),
    )
    out_specs = P(("dp", "seq"), None, None)
    return jax.shard_map(shards, mesh=mesh, in_specs=in_specs, out_specs=out_specs, check_vma=False)
```
